32 devices in a mesh: ctx: 32 (over z, y, x, core), dp: 1.
Axes of the slice: x: 2, y: 2, z: 4, core: 2. Of those that a mesh axis runs over, the one named last changes fastest.
Arguments:
- tokens: bfloat16 [1, 8192, 768], P('dp', 'ctx'), may hold values from -40 to 40
- cotangent: bfloat16 [1, 8192, 768], P('dp', 'ctx'), may hold values from -200 to 200
- norm_gain: float32 [768], replicated, may hold values from 0.1 to 1.9
- conv_weight: bfloat16 [3, 768, 768], P(None, 'ctx'), may hold values from -0.125 to 0.125
- up_weight: bfloat16 [768, 1152], P('ctx'), may hold values from -0.21875 to 0.21875
- down_weight: bfloat16 [1152, 768], P('ctx'), may hold values from -0.1875 to 0.1875
- contig_first_bins: int32 [4], replicated, may hold values from 0 to 6655, as said below
Outputs:
- output: bfloat16 [1, 8192, 768], P('dp', 'ctx')
- input_grad: bfloat16 [1, 8192, 768], P('dp', 'ctx')
- down_grad: float32 [1152, 768], P('ctx', 'dp')
- gain_grad: float32 [768], P('dp')
The draws below stay inside these ranges and needn't reach their ends.
Inputs may be any that keep to these rules, and one draw needn't show every extreme that they name: contig_first_bins[0] = 0; the starts increase strictly, consecutive ones at least 1024 bins apart; the last contig starts at 6655.
All inputs are finite; a program needn't handle non-finite values.
Results may differ from the reference program's by a relative error of at most 0.0054.
Values may be sent and summed in bfloat16 or wider, within the bound.
No kernel may reach another device: no remote copies, remote signals or barrier semaphores. Data moves between devices by JAX's collectives and lax.ppermute only.
A program may use at most 64 MiB of HBM per device.

```python
import math
import jax
import jax.numpy as jnp
from jax import lax

BLOCK_CHANNELS = 768
FF = 1152
DILATION_BINS = 64
BINS_DEV = 256
TOTAL = 8192
BATCH = 1
CONTIGS = 4


def draw_tokens(key, part):
    noise_key, row_key, chan_key = jax.random.split(key, 3)
    row_scale = jnp.exp(jax.random.uniform(row_key, (BATCH, TOTAL, 1), jnp.float32, math.log(0.3), math.log(3.0)))
    chan_scale = jnp.exp(jax.random.uniform(chan_key, (1, 1, BLOCK_CHANNELS), jnp.float32, math.log(0.3), math.log(3.0)))
    base = jax.random.truncated_normal(noise_key, -4.0, 4.0, (BATCH, TOTAL, BLOCK_CHANNELS), jnp.float32)
    return (base * row_scale * chan_scale).astype(jnp.bfloat16)


def draw_cotangent(key, part):
    noise_key = jax.random.fold_in(key, 0)
    heavy_key = jax.random.fold_in(key, 2)
    along = jnp.arange(TOTAL, dtype=jnp.float32)[None, :, None] / TOTAL
    segment_count = TOTAL // BINS_DEV
    chosen = jax.random.randint(heavy_key, (BATCH, 1), 0, segment_count, jnp.int32)
    segment_of_bin = jnp.arange(TOTAL, dtype=jnp.int32)[None, :] // BINS_DEV
    heavy = jnp.where(segment_of_bin == chosen, 5.0, 1.0).astype(jnp.float32)[:, :, None]
    base = jax.random.truncated_normal(noise_key, -4.0, 4.0, (BATCH, TOTAL, BLOCK_CHANNELS), jnp.float32)
    rising = 1.0 + 2.0 * along
    return (base * rising * heavy).astype(jnp.bfloat16)


def draw_contig_first_bins(key, part):
    spacing = TOTAL // CONTIGS
    jitter = jax.random.randint(key, (CONTIGS,), -2 * BINS_DEV, 2 * BINS_DEV, jnp.int32)
    counter = jnp.arange(CONTIGS, dtype=jnp.int32)
    starts = counter * spacing + jitter
    last_start = TOTAL - 6 * BINS_DEV - 1
    starts = jnp.where(counter == CONTIGS - 1, last_start, starts)
    return jnp.where(counter == 0, 0, starts).astype(jnp.int32)


def block_scale(own_key, shape, shards, least, largest):
    factor_of, own = 1.0, jax.random.fold_in(own_key, 6)
    for axis_at, blocks in shards:
        heights = jnp.exp(jax.random.uniform(jax.random.fold_in(own, axis_at), (blocks,), jnp.float32, least / len(shards), largest / len(shards)))
        factor_of = factor_of * jnp.repeat(heights, shape[axis_at] // blocks).reshape([-1 if axis == axis_at else 1 for axis in range(len(shape))])
    return factor_of


def gaussian(rng, dims, spread, most, pieces=(), held_as=jnp.bfloat16):
    array = spread * jax.random.normal(rng, dims, jnp.float32)
    if pieces:
        array = array * block_scale(rng, dims, pieces, -0.22, 0.18)
    return jnp.clip(array, -most, most).astype(held_as)


def setup_inputs(seed: int = 0) -> dict:
    arg_keys = jax.random.split(jax.random.key(seed), 8)
    tokens = draw_tokens(jax.random.fold_in(arg_keys[7], 71), 0)
    cotangent = draw_cotangent(jax.random.fold_in(arg_keys[7], 71), 0)
    norm_gain = jnp.clip(1.0 + 0.18 * jax.random.normal(arg_keys[2], (BLOCK_CHANNELS,), jnp.float32), 0.1, 1.9)
    conv_weight = gaussian(arg_keys[3], (3, BLOCK_CHANNELS, BLOCK_CHANNELS), (3 * BLOCK_CHANNELS) ** -0.5, 0.125, ((1, 32),))
    up_weight = gaussian(arg_keys[4], (BLOCK_CHANNELS, FF), BLOCK_CHANNELS ** -0.5, 0.21875, ((0, 32),))
    down_weight = gaussian(arg_keys[5], (FF, BLOCK_CHANNELS), FF ** -0.5, 0.1875, ((0, 32),))
    contig_first_bins = draw_contig_first_bins(jax.random.fold_in(arg_keys[7], 71), 0)
    return {"tokens": tokens, "cotangent": cotangent, "norm_gain": norm_gain, "conv_weight": conv_weight, "up_weight": up_weight, "down_weight": down_weight, "contig_first_bins": contig_first_bins}


root_half = 0.7071067811865476
inv_root_two_pi = 0.3989422804014327

def segment_lookup(bin_position, contig_first_bins):
    return lax.optimization_barrier(jnp.sum((contig_first_bins[None, :] <= bin_position[:, None]).astype(jnp.int32), axis=1))

def tap_masks(bin_position, contig_first_bins, overall_bin_count):
    current_segment = segment_lookup(bin_position, contig_first_bins)
    preceding_segment = segment_lookup(bin_position - DILATION_BINS, contig_first_bins)
    following_segment = segment_lookup(bin_position + DILATION_BINS, contig_first_bins)
    left_valid_mask = jnp.logical_and(bin_position >= DILATION_BINS, preceding_segment == current_segment)
    right_valid_mask = jnp.logical_and(bin_position + DILATION_BINS < overall_bin_count, following_segment == current_segment)
    return (left_valid_mask.astype(jnp.bfloat16)[:, None], right_valid_mask.astype(jnp.bfloat16)[:, None])

def gelu_value(pre_value):
    return 0.5 * pre_value * (1.0 + lax.erf(pre_value * root_half))

def gelu_slope(pre_value):
    return 0.5 * (1.0 + lax.erf(pre_value * root_half)) + pre_value * jnp.exp(-0.5 * pre_value * pre_value) * inv_root_two_pi

def one_sequence(tokens, cotangent, norm_gain, conv_weight, up_weight, down_weight, left_valid_mask, right_valid_mask):
    tok_float = tokens.astype(jnp.float32)
    inverse = lax.rsqrt(lax.optimization_barrier(jnp.mean(tok_float * tok_float, axis=1, keepdims=True)) + 1e-05)
    scaled = tok_float * inverse
    normalized_input = (scaled * norm_gain).astype(jnp.bfloat16)
    empty_padding_rows = jnp.zeros((DILATION_BINS, BLOCK_CHANNELS), jnp.bfloat16)
    preceding_value = jnp.concatenate([empty_padding_rows, normalized_input[:-DILATION_BINS]], axis=0) * left_valid_mask
    following_tap = jnp.concatenate([normalized_input[DILATION_BINS:], empty_padding_rows], axis=0) * right_valid_mask
    stacked = jnp.concatenate([preceding_value, normalized_input, following_tap], axis=1)
    conv_out = jnp.dot(stacked, conv_weight.reshape(3 * BLOCK_CHANNELS, BLOCK_CHANNELS), preferred_element_type=jnp.float32)
    mixed_sum = tok_float + conv_out
    pre_act = jnp.dot(mixed_sum.astype(jnp.bfloat16), up_weight, preferred_element_type=jnp.float32)
    hidden = gelu_value(pre_act).astype(jnp.bfloat16)
    output = (mixed_sum + jnp.dot(hidden, down_weight, preferred_element_type=jnp.float32)).astype(jnp.bfloat16)
    hidden_grad = jnp.dot(cotangent, down_weight.T, preferred_element_type=jnp.float32)
    pre_grad = (hidden_grad * gelu_slope(pre_act)).astype(jnp.bfloat16)
    mixed_grad = cotangent.astype(jnp.float32) + jnp.dot(pre_grad, up_weight.T, preferred_element_type=jnp.float32)
    convolution_gradient = mixed_grad.astype(jnp.bfloat16)
    following_gradient = jnp.concatenate([convolution_gradient[DILATION_BINS:], empty_padding_rows], axis=0) * right_valid_mask
    preceding_gradient = jnp.concatenate([empty_padding_rows, convolution_gradient[:-DILATION_BINS]], axis=0) * left_valid_mask
    back_stack = jnp.concatenate([following_gradient, convolution_gradient, preceding_gradient], axis=1)
    back_weight = jnp.transpose(conv_weight, (0, 2, 1)).reshape(3 * BLOCK_CHANNELS, BLOCK_CHANNELS)
    normed_grad = jnp.dot(back_stack, back_weight, preferred_element_type=jnp.float32)
    scaled_grad = normed_grad * norm_gain
    inner_mean = lax.optimization_barrier(jnp.mean(scaled_grad * scaled, axis=1, keepdims=True))
    input_grad = (mixed_grad + inverse * (scaled_grad - scaled * inner_mean)).astype(jnp.bfloat16)
    gain_term = lax.optimization_barrier(jnp.sum(normed_grad * scaled, axis=0))
    down_term = jnp.dot(hidden.T, cotangent, preferred_element_type=jnp.float32)
    return (output, input_grad, gain_term, down_term)

def reference(tokens, cotangent, norm_gain, conv_weight, up_weight, down_weight, contig_first_bins):
    bin_position = jnp.arange(TOTAL, dtype=jnp.int32)
    left_valid_mask, right_valid_mask = tap_masks(bin_position, contig_first_bins, TOTAL)

    def per_row(row_pair):
        return one_sequence(row_pair[0], row_pair[1], norm_gain, conv_weight, up_weight, down_weight, left_valid_mask, right_valid_mask)
    outputs, input_grads, gain_terms, down_terms = lax.map(per_row, (tokens, cotangent))
    factor = float(BATCH * TOTAL) ** (-0.5)
    down_grad = lax.optimization_barrier(jnp.sum(down_terms, axis=0)) * factor
    gain_grad = lax.optimization_barrier(jnp.sum(gain_terms, axis=0)) * factor
    return (outputs, input_grads, down_grad, gain_grad)
```

```python
import jax
import jax.numpy as jnp
from jax import lax
from jax.experimental import pallas as pl
from jax.experimental.pallas import tpu as pltpu
from jax.sharding import PartitionSpec as P

DILATION_BINS = 64


root_half = 0.7071067811865476
inv_root_two_pi = 0.3989422804014327


def with_halo(value, sides, width):
    for axis, dim in sides:
        devices, length = (lax.axis_size(axis), value.shape[dim])
        up = [(i, (i + 1) % devices) for i in range(devices - 1)]
        down = [(j, i) for i, j in up]
        last = lax.slice_in_dim(value, length - width, length, axis=dim)
        leading = lax.slice_in_dim(value, 0, width, axis=dim)
        before = lax.ppermute(last, axis, up)
        after = lax.ppermute(leading, axis, down)
        value = jnp.concatenate([before, value, after], axis=dim)
    return value


def segment_lookup(bin_position, contig_first_bins):
    return jnp.sum((contig_first_bins[None, :] <= bin_position[:, None]).astype(jnp.int32), axis=1)


def tap_masks(bin_position, contig_first_bins, overall_bin_count):
    current_segment = segment_lookup(bin_position, contig_first_bins)
    preceding_segment = segment_lookup(bin_position - DILATION_BINS, contig_first_bins)
    following_segment = segment_lookup(bin_position + DILATION_BINS, contig_first_bins)
    left_valid_mask = jnp.logical_and(
        bin_position >= DILATION_BINS, preceding_segment == current_segment
    )
    right_valid_mask = jnp.logical_and(
        bin_position + DILATION_BINS < overall_bin_count, following_segment == current_segment
    )
    return (
        left_valid_mask.astype(jnp.bfloat16)[:, None],
        right_valid_mask.astype(jnp.bfloat16)[:, None],
    )


def gelu_value(pre_value):
    return 0.5 * pre_value * (1.0 + lax.erf(pre_value * root_half))


def gelu_slope(pre_value):
    return (
        0.5 * (1.0 + lax.erf(pre_value * root_half))
        + pre_value * jnp.exp(-0.5 * pre_value * pre_value) * inv_root_two_pi
    )


def ring_order(squares):
    return list(range(0, squares, 2)) + list(range(1, squares, 2))[::-1]


def swap(value, mask):
    devices = lax.axis_size("ctx")
    return lax.ppermute(value, "ctx", [(i, i ^ mask) for i in range(devices)])


def ring(value, steps):
    devices = lax.axis_size("ctx")
    order = ring_order(devices // 8)
    count = len(order)
    to = {order[i]: order[(i + steps) % count] for i in range(count)}
    return lax.ppermute(value, "ctx", [(i, i % 8 + 8 * to[i // 8]) for i in range(devices)])


def place():
    me = lax.axis_index("ctx")
    return me % 2, (me // 2) % 2, (me // 4) % 2, me // 8


def square_at(mine, steps, squares):
    order = ring_order(squares)
    at = jnp.int32(0)
    for i, square in enumerate(order):
        at = at + jnp.where(mine == square, order[(i + steps) % squares], 0).astype(jnp.int32)
    return at


def gather_pieces(piece):
    squares = lax.axis_size("ctx") // 8
    held = [piece]
    for _ in range(squares - 1):
        held.append(ring(held[-1], 1))
    column = jnp.stack(held)
    half = squares // 2
    by_x, by_y = swap(column, 2), swap(column, 4)
    far_first, far_second = swap(by_x[:half], 4), swap(by_y[half:], 2)
    pieces = [column, by_x, by_y, far_first, far_second]
    return pieces + [swap(p, 1) for p in pieces]


def piece_slots(squares):
    half = squares // 2
    for core in range(2):
        for k in range(squares):
            yield 5 * core, k, k, 0, 0, core
            yield 5 * core + 1, k, k, 0, 1, core
            yield 5 * core + 2, k, k, 1, 0, core
            if k < half:
                yield 5 * core + 3, k, k, 1, 1, core
            else:
                yield 5 * core + 4, k - half, k, 1, 1, core


VMEM = pl.BlockSpec(memory_space=pltpu.VMEM)
PARAMS = pltpu.CompilerParams(vmem_limit_bytes=48 * 1024 * 1024)


def assemble_rows(pieces, lead):
    squares = lax.axis_size("ctx") // 8
    rows, width = pieces[0].shape[-2:]
    flat = [p.reshape(p.shape[0], lead, rows, width) for p in pieces]

    def kernel(*refs):
        out = refs[-1]
        core, x, y, z = place()
        for piece, slot, back, dy, dx, dc in piece_slots(squares):
            source = square_at(z, -back, squares)
            for t in range(lead):
                out[t, source, y ^ dy, x ^ dx, core ^ dc] = refs[piece][slot, t]

    out = pl.pallas_call(
        kernel,
        out_shape=jax.ShapeDtypeStruct((lead, squares, 2, 2, 2, rows, width), flat[0].dtype),
        in_specs=[VMEM] * len(flat),
        out_specs=VMEM,
        compiler_params=PARAMS,
    )(*flat)
    return out.reshape(lead, squares * 8 * rows, width)


def assemble_columns(pieces):
    squares = lax.axis_size("ctx") // 8
    rows, width = pieces[0].shape[-2:]

    def kernel(*refs):
        out = refs[-1]
        core, x, y, z = place()
        for piece, slot, back, dy, dx, dc in piece_slots(squares):
            source = square_at(z, -back, squares)
            columns = pl.ds(pl.multiple_of((core ^ dc) * width, 128), width)
            out[source, y ^ dy, x ^ dx, :, columns] = refs[piece][slot]

    out = pl.pallas_call(
        kernel,
        out_shape=jax.ShapeDtypeStruct((squares, 2, 2, rows, 2 * width), pieces[0].dtype),
        in_specs=[VMEM] * len(pieces),
        out_specs=VMEM,
        compiler_params=PARAMS,
    )(*pieces)
    return out.reshape(squares * 4 * rows, 2 * width)


def halves_by_core(value):
    width = value.shape[-1] // 2
    first = lax.axis_index("ctx") % 2 == 0
    left, right = value[..., :width], value[..., width:]
    return jnp.where(first, left, right), jnp.where(first, right, left)


def in_core_order(own, other, axis):
    first = lax.axis_index("ctx") % 2 == 0
    return jnp.where(
        first, jnp.concatenate([own, other], axis), jnp.concatenate([other, own], axis)
    )


def gather_weights(conv_weight, up_weight, down_weight):
    conv_pieces = gather_pieces(conv_weight)
    up_pieces = gather_pieces(up_weight)
    own, other = halves_by_core(down_weight)
    down_pieces = gather_pieces(in_core_order(own, swap(other, 1), 0))
    taps = conv_weight.shape[0]
    return (
        assemble_rows(conv_pieces, taps),
        assemble_rows(up_pieces, 1)[0],
        assemble_columns(down_pieces),
    )


def relative_blocks(total):
    squares = lax.axis_size("ctx") // 8
    rows, width = total.shape[0] // (4 * squares), total.shape[1] // 2
    blocks = total.reshape(squares, 2, 2, rows, 2 * width)

    def kernel(blocks_ref, keep_ref, send_ref):
        core, x, y, z = place()
        keep = pl.ds(pl.multiple_of(core * width, 128), width)
        send = pl.ds(pl.multiple_of((1 - core) * width, 128), width)
        for k in range(squares):
            at = square_at(z, k, squares)
            for dy in range(2):
                for dx in range(2):
                    keep_ref[k, dy, dx] = blocks_ref[at, y ^ dy, x ^ dx, :, keep]
                    send_ref[k, dy, dx] = blocks_ref[at, y ^ dy, x ^ dx, :, send].astype(
                        jnp.bfloat16
                    )

    shape = (squares, 2, 2, rows, width)
    return pl.pallas_call(
        kernel,
        out_shape=(
            jax.ShapeDtypeStruct(shape, jnp.float32),
            jax.ShapeDtypeStruct(shape, jnp.bfloat16),
        ),
        in_specs=[VMEM],
        out_specs=(VMEM, VMEM),
        compiler_params=PARAMS,
    )(blocks)


def scatter_sum(total):
    squares = lax.axis_size("ctx") // 8
    half = squares // 2
    keep, send = relative_blocks(total)
    chip = keep + swap(send, 1).astype(jnp.float32)
    low = lambda v: v.astype(jnp.bfloat16)
    wide = lambda v: v.astype(jnp.float32)
    first = chip[:half, :, 0] + wide(swap(low(chip[:half, :, 1]), 2))
    second = chip[half:, 0] + wide(swap(low(chip[half:, 1]), 4))
    first = first[:, 0] + wide(swap(low(first[:, 1]), 4))
    second = second[:, 0] + wide(swap(low(second[:, 1]), 2))
    own = first[0]
    for k in range(1, squares):
        piece = first[k] if k < half else second[k - half]
        own = own + wide(ring(low(piece), k))
    rows = own.shape[0] // 2
    is_first = lax.axis_index("ctx") % 2 == 0
    mine = jnp.where(is_first, own[:rows], own[rows:])
    theirs = jnp.where(is_first, own[rows:], own[:rows])
    return in_core_order(mine, swap(theirs, 1), 1)


def sum_all(value):
    squares = lax.axis_size("ctx") // 8
    for mask in (1, 2, 4):
        value = value + swap(value, mask)
    own = value
    for k in range(1, squares):
        value = value + ring(own, k)
    return value


def body(tokens, cotangent, norm_gain, conv_weight, up_weight, down_weight, contig_first_bins):
    seq_count, bin_count, feat_width = tokens.shape
    ctx_count = lax.axis_size("ctx")
    data_count = lax.axis_size("dp")
    conv_full, up_full, down_full = gather_weights(conv_weight, up_weight, down_weight)
    bin_position = lax.axis_index("ctx") * bin_count + jnp.arange(bin_count, dtype=jnp.int32)
    left_valid_mask, right_valid_mask = tap_masks(
        bin_position, contig_first_bins, ctx_count * bin_count
    )
    tok_float = tokens.astype(jnp.float32)
    inverse = lax.rsqrt(jnp.mean(tok_float * tok_float, axis=2, keepdims=True) + 1e-05)
    scaled = tok_float * inverse
    normalized_input = (scaled * norm_gain).astype(jnp.bfloat16)
    padded_input = with_halo(normalized_input, (("ctx", 1),), DILATION_BINS)
    preceding_value = padded_input[:, :bin_count] * left_valid_mask
    following_tap = padded_input[:, 2 * DILATION_BINS :] * right_valid_mask
    stacked = jnp.concatenate([preceding_value, normalized_input, following_tap], axis=2).reshape(
        seq_count * bin_count, 3 * feat_width
    )
    conv_out = jnp.dot(
        stacked, conv_full.reshape(3 * feat_width, feat_width), preferred_element_type=jnp.float32
    )
    mixed_sum = tok_float.reshape(-1, feat_width) + conv_out
    pre_act = jnp.dot(mixed_sum.astype(jnp.bfloat16), up_full, preferred_element_type=jnp.float32)
    hidden = gelu_value(pre_act).astype(jnp.bfloat16)
    output = (mixed_sum + jnp.dot(hidden, down_full, preferred_element_type=jnp.float32)).astype(
        jnp.bfloat16
    )
    grad_flat = cotangent.reshape(-1, feat_width)
    total = lax.dot_general(
        hidden, grad_flat, (((0,), (0,)), ((), ())), preferred_element_type=jnp.float32
    )
    hidden_grad = lax.dot_general(
        grad_flat, down_full, (((1,), (1,)), ((), ())), preferred_element_type=jnp.float32
    )
    pre_grad = (hidden_grad * gelu_slope(pre_act)).astype(jnp.bfloat16)
    mixed_grad = grad_flat.astype(jnp.float32) + lax.dot_general(
        pre_grad, up_full, (((1,), (1,)), ((), ())), preferred_element_type=jnp.float32
    )
    convolution_gradient = mixed_grad.astype(jnp.bfloat16).reshape(seq_count, bin_count, feat_width)
    padded_gradient = with_halo(convolution_gradient, (("ctx", 1),), DILATION_BINS)
    preceding_gradient = padded_gradient[:, :bin_count] * left_valid_mask
    following_gradient = padded_gradient[:, 2 * DILATION_BINS :] * right_valid_mask
    back_stack = jnp.stack(
        [following_gradient, convolution_gradient, preceding_gradient], axis=2
    ).reshape(seq_count * bin_count, 3, feat_width)
    normed_grad = lax.dot_general(
        back_stack, conv_full, (((1, 2), (0, 2)), ((), ())), preferred_element_type=jnp.float32
    )
    scaled_flat = scaled.reshape(-1, feat_width)
    scaled_grad = normed_grad * norm_gain
    inner_mean = jnp.mean(scaled_grad * scaled_flat, axis=1, keepdims=True)
    input_grad = (
        mixed_grad + inverse.reshape(-1, 1) * (scaled_grad - scaled_flat * inner_mean)
    ).astype(jnp.bfloat16)
    gain_term = jnp.sum(normed_grad * scaled_flat, axis=0)
    factor = float(ctx_count * data_count * bin_count * seq_count) ** (-0.5)
    width_part = feat_width // data_count
    down_part = scatter_sum(total)
    gain_all = sum_all(gain_term)
    if data_count > 1:
        down_part = lax.psum_scatter(down_part, "dp", scatter_dimension=1, tiled=True)
        gain_all = lax.psum(gain_all, "dp")
    gain_part = lax.dynamic_slice_in_dim(gain_all, lax.axis_index("dp") * width_part, width_part)
    return (
        output.reshape(tokens.shape),
        input_grad.reshape(tokens.shape),
        down_part * factor,
        gain_part * factor,
    )


def solution(mesh):
    placed = (
        P("dp", "ctx", None),
        P("dp", "ctx", None),
        P(),
        P(None, "ctx", None),
        P("ctx", None),
        P("ctx", None),
        P(),
    )
    return jax.shard_map(
        body,
        mesh=mesh,
        in_specs=placed,
        out_specs=(P("dp", "ctx", None), P("dp", "ctx", None), P("ctx", "dp"), P("dp")),
        check_vma=False,
    )
```

```python
import jax
import jax.numpy as jnp
from jax import lax
from jax.experimental import pallas as pl
from jax.experimental.pallas import tpu as pltpu
from jax.sharding import PartitionSpec as P

DILATION_BINS = 64


root_half = 0.7071067811865476
inv_root_two_pi = 0.3989422804014327


def swap(value, mask):
    devices = lax.axis_size("ctx")
    return lax.ppermute(value, "ctx", [(i, i ^ mask) for i in range(devices)])


def place():
    me = lax.axis_index("ctx")
    return me % 2, (me // 2) % 2, (me // 4) % 2, me // 8


def after(value, *others):
    return lax.optimization_barrier((value,) + others)[0]


VMEM = pl.BlockSpec(memory_space=pltpu.VMEM)
PARAMS = pltpu.CompilerParams(vmem_limit_bytes=20 * 1024 * 1024)

SMEM = pl.BlockSpec(memory_space=pltpu.SMEM)


def call(kernel, outs, *args, smem=(), scratch=(), cost=1):
    shapes = [jax.ShapeDtypeStruct(shape, dtype) for shape, dtype in outs]
    return pl.pallas_call(
        kernel,
        out_shape=shapes,
        in_specs=[SMEM if i in smem else VMEM for i in range(len(args))],
        out_specs=[VMEM] * len(shapes),
        scratch_shapes=list(scratch),
        compiler_params=PARAMS,
        cost_estimate=pl.CostEstimate(flops=1, bytes_accessed=cost, transcendentals=0),
    )(*args)


def segment_of(position, starts_ref):
    segment = jnp.zeros_like(position)
    for i in range(starts_ref.shape[0]):
        segment = segment + jnp.where(position >= starts_ref[i], 1, 0)
    return segment


def masks_at(first, rows, starts_ref, overall):
    position = first + lax.broadcasted_iota(jnp.int32, (rows, 1), 0)
    segment = segment_of(position, starts_ref)
    left = (position >= DILATION_BINS) & (segment_of(position - DILATION_BINS, starts_ref) == segment)
    right = (position + DILATION_BINS < overall) & (
        segment_of(position + DILATION_BINS, starts_ref) == segment
    )
    return left, right


def column_blocks(width):
    step = 384 if width % 384 == 0 else width
    return [slice(at, at + step) for at in range(0, width, step)]


def prepare(before, tokens, after_, gain, starts):
    seqs, bins, width = tokens.shape
    reach = DILATION_BINS
    overall = bins * lax.axis_size("ctx")

    def kernel(before_ref, tokens_ref, after_ref, gain_ref, starts_ref, taps_ref, scaled_ref, inverse_ref):
        first = lax.axis_index("ctx") * bins - reach
        left, right = masks_at(first, bins + 2 * reach, starts_ref, overall)
        for s in range(seqs):
            parts = []
            for ref in (before_ref, tokens_ref, after_ref):
                value = (tokens_ref[s] if ref is tokens_ref else ref[s, : 2 * reach]).astype(jnp.float32)
                inverse = lax.rsqrt(jnp.mean(value * value, axis=1, keepdims=True) + 1e-05)
                scaled = value * inverse
                if ref is tokens_ref:
                    scaled_ref[s] = scaled
                    inverse_ref[s] = inverse
                parts.append(scaled * gain_ref[...])
            normed = jnp.concatenate(parts, axis=0)
            rows = bins + 2 * reach
            taps_ref[s, :, :width] = jnp.where(left, normed[:rows], 0.0).astype(jnp.bfloat16)
            taps_ref[s, :, width : 2 * width] = normed[reach : reach + rows].astype(jnp.bfloat16)
            taps_ref[s, :, 2 * width :] = jnp.where(right, normed[2 * reach :], 0.0).astype(
                jnp.bfloat16
            )

    return call(
        kernel,
        [
            ((seqs, bins + 2 * reach, 3 * width), jnp.bfloat16),
            ((seqs, bins, width), jnp.float32),
            ((seqs, bins, 1), jnp.float32),
        ],
        before,
        tokens,
        after_,
        gain,
        starts,
        smem=(4,),
    )


def convolve(taps, before, tokens, after_, conv):
    seqs, bins, width = tokens.shape
    reach = DILATION_BINS
    rows = bins + 2 * reach

    def kernel(taps_ref, before_ref, tokens_ref, after_ref, conv_ref, mixed_ref):
        for s in range(seqs):
            for at in column_blocks(width):
                total = jnp.dot(
                    taps_ref[s], conv_ref[:, at], preferred_element_type=jnp.float32
                )
                mixed_ref[s, :reach, at] = total[:reach] + before_ref[s, reach : 2 * reach, at].astype(jnp.float32)
                mixed_ref[s, reach : reach + bins, at] = total[reach : reach + bins] + tokens_ref[
                    s, :, at
                ].astype(jnp.float32)
                mixed_ref[s, reach + bins :, at] = total[reach + bins :] + after_ref[
                    s, :reach, at
                ].astype(jnp.float32)

    return call(
        kernel,
        [((seqs, rows, width), jnp.float32)],
        taps,
        before,
        tokens,
        after_,
        conv.reshape(-1, width),
    )[0]


def expand(mixed, up, cotangent):
    seqs, bins, width = cotangent.shape
    hidden_width = up.shape[1]
    reach = DILATION_BINS

    def kernel(mixed_ref, up_ref, cotangent_ref, pre_ref, share_ref, hidden_ref, total_ref):
        for s in range(seqs):
            low = mixed_ref[s, reach : reach + bins].astype(jnp.bfloat16)
            for at in column_blocks(hidden_width):
                pre = jnp.dot(low, up_ref[:, at], preferred_element_type=jnp.float32)
                share = 0.5 * (1.0 + lax.erf(pre * root_half))
                hidden = (pre * share).astype(jnp.bfloat16)
                pre_ref[s, :, at] = pre
                share_ref[s, :, at] = share
                hidden_ref[s, :, at] = hidden
                term = lax.dot_general(
                    hidden,
                    cotangent_ref[s],
                    (((0,), (0,)), ((), ())),
                    preferred_element_type=jnp.float32,
                )
                if s == 0:
                    total_ref[at, :] = term
                else:
                    total_ref[at, :] += term

    return call(
        kernel,
        [
            ((seqs, bins, hidden_width), jnp.float32),
            ((seqs, bins, hidden_width), jnp.float32),
            ((seqs, bins, hidden_width), jnp.bfloat16),
            ((hidden_width, width), jnp.float32),
        ],
        mixed,
        up,
        cotangent,
    )


def slopes(mixed, up, pre, share):
    seqs, bins, hidden_width = pre.shape
    reach = DILATION_BINS
    rows = bins + 2 * reach

    def bell(value):
        return value * jnp.exp(-0.5 * value * value) * inv_root_two_pi

    def kernel(mixed_ref, up_ref, pre_ref, share_ref, slope_ref):
        for s in range(seqs):
            edges = jnp.concatenate(
                [mixed_ref[s, :reach], mixed_ref[s, reach + bins :]], axis=0
            ).astype(jnp.bfloat16)
            for at in column_blocks(hidden_width):
                edge = jnp.dot(edges, up_ref[:, at], preferred_element_type=jnp.float32)
                slope = 0.5 * (1.0 + lax.erf(edge * root_half)) + bell(edge)
                slope_ref[s, :reach, at] = slope[:reach]
                slope_ref[s, reach : reach + bins, at] = share_ref[s, :, at] + bell(pre_ref[s, :, at])
                slope_ref[s, reach + bins :, at] = slope[reach:]

    return call(
        kernel,
        [((seqs, rows, hidden_width), jnp.float32)],
        mixed,
        up,
        pre,
        share,
    )[0]


def backward(before, cotangent, after_, slope, down, up, conv, scaled, inverse, gain, starts):
    seqs, bins, width = cotangent.shape
    hidden_width = up.shape[1]
    reach = DILATION_BINS
    rows = bins + 2 * reach
    overall = bins * lax.axis_size("ctx")
    by_rows = (((1,), (1,)), ((), ()))

    def kernel(
        before_ref,
        cotangent_ref,
        after_ref,
        slope_ref,
        down_ref,
        up_ref,
        conv_ref,
        scaled_ref,
        inverse_ref,
        gain_ref,
        starts_ref,
        grad_ref,
        gain_term_ref,
        pre_grad,
        mixed_grad,
    ):
        first = lax.axis_index("ctx") * bins
        left, right = masks_at(first, bins, starts_ref, overall)
        for s in range(seqs):
            cot = jnp.concatenate(
                [before_ref[s, 2 * reach :], cotangent_ref[s], after_ref[s, 2 * reach :]], axis=0
            )
            for at in column_blocks(hidden_width):
                hidden_grad = lax.dot_general(
                    cot, down_ref[at, :], by_rows, preferred_element_type=jnp.float32
                )
                pre_grad[:, at] = (hidden_grad * slope_ref[s, :, at]).astype(jnp.bfloat16)
            for at in column_blocks(width):
                mixed_grad[:, at] = cot[:, at].astype(jnp.float32) + lax.dot_general(
                    pre_grad[...], up_ref[at, :], by_rows, preferred_element_type=jnp.float32
                )
            following = jnp.where(right, mixed_grad[2 * reach :, :], 0.0).astype(jnp.bfloat16)
            center = mixed_grad[reach : reach + bins, :].astype(jnp.bfloat16)
            preceding = jnp.where(left, mixed_grad[:bins, :], 0.0).astype(jnp.bfloat16)
            normed_grad = (
                lax.dot_general(following, conv_ref[0], by_rows, preferred_element_type=jnp.float32)
                + lax.dot_general(center, conv_ref[1], by_rows, preferred_element_type=jnp.float32)
                + lax.dot_general(preceding, conv_ref[2], by_rows, preferred_element_type=jnp.float32)
            )
            scaled = scaled_ref[s]
            term = jnp.sum(normed_grad * scaled, axis=0, keepdims=True)
            if s == 0:
                gain_term_ref[...] = term
            else:
                gain_term_ref[...] += term
            scaled_grad = normed_grad * gain_ref[...]
            inner = jnp.mean(scaled_grad * scaled, axis=1, keepdims=True)
            grad_ref[s] = (
                mixed_grad[reach : reach + bins, :]
                + inverse_ref[s] * (scaled_grad - scaled * inner)
            ).astype(jnp.bfloat16)

    return call(
        kernel,
        [((seqs, bins, width), jnp.bfloat16), ((1, width), jnp.float32)],
        before,
        cotangent,
        after_,
        slope,
        down,
        up,
        conv,
        scaled,
        inverse,
        gain,
        starts,
        smem=(10,),
        scratch=[
            pltpu.VMEM((rows, hidden_width), jnp.bfloat16),
            pltpu.VMEM((rows, width), jnp.float32),
        ],
    )


def project(mixed, hidden, down):
    seqs, bins, _ = hidden.shape
    width = down.shape[1]
    reach = DILATION_BINS

    def kernel(mixed_ref, hidden_ref, down_ref, out_ref):
        for s in range(seqs):
            for at in column_blocks(width):
                out_ref[s, :, at] = (
                    mixed_ref[s, reach : reach + bins, at]
                    + jnp.dot(hidden_ref[s], down_ref[:, at], preferred_element_type=jnp.float32)
                ).astype(jnp.bfloat16)

    return call(
        kernel,
        [((seqs, bins, width), jnp.bfloat16)],
        mixed,
        hidden,
        down,
    )[0]


def stack(pieces):
    def kernel(*refs):
        for i in range(len(pieces)):
            refs[-1][i] = refs[i][...]

    return call(kernel, [((len(pieces),) + pieces[0].shape, pieces[0].dtype)], *pieces)[0]


def join(*pieces):
    ends = [sum(piece.shape[0] for piece in pieces[: i + 1]) for i in range(len(pieces))]

    def kernel(*refs):
        for ref, end in zip(refs[:-1], ends):
            refs[-1][end - ref.shape[0] : end] = ref[...]

    return call(kernel, [((ends[-1],) + pieces[0].shape[1:], pieces[0].dtype)], *pieces)[0]


def join_rows(pieces, rows):
    ends = [sum(piece.shape[0] for piece in pieces[: i + 1]) for i in range(len(pieces))]
    held, width = pieces[0].shape[1:]

    def kernel(*refs):
        for ref, end in zip(refs[:-2], ends):
            refs[-2][end - ref.shape[0] : end] = ref[:, :rows]
            refs[-1][end - ref.shape[0] : end] = ref[:, rows:]

    shapes = [(ends[-1], rows, width), (ends[-1], held - rows, width)]
    return call(kernel, [(shape, pieces[0].dtype) for shape in shapes], *pieces)


def neighbours(tokens, cotangent):
    devices = lax.axis_size("ctx")
    pairs = [(i, i + 1) for i in range(1, devices - 1, 2)]
    pairs += [(j, i) for i, j in pairs]
    far, near = 2 * DILATION_BINS, DILATION_BINS
    seqs, bins, width = tokens.shape

    def cut(tokens_ref, cotangent_ref, last_ref, leading_ref):
        last_ref[:, :far] = tokens_ref[:, bins - far :]
        last_ref[:, far:] = cotangent_ref[:, bins - near :]
        leading_ref[:, :far] = tokens_ref[:, :far]
        leading_ref[:, far:] = cotangent_ref[:, :near]

    def kernel(tokens_ref, cotangent_ref, inner_ref, outer_ref):
        is_first = lax.axis_index("ctx") % 2 == 0

        @pl.when(is_first)
        def _():
            cut(tokens_ref, cotangent_ref, inner_ref, outer_ref)

        @pl.when(jnp.logical_not(is_first))
        def _():
            cut(tokens_ref, cotangent_ref, outer_ref, inner_ref)

    edge = ((seqs, far + near, width), tokens.dtype)
    inner, outer = call(kernel, [edge, edge], tokens, cotangent)
    return inner, lax.ppermute(outer, "ctx", pairs)


def in_order(inner, outer):
    def kernel(inner_ref, outer_ref, before_ref, after_ref):
        is_first = lax.axis_index("ctx") % 2 == 0

        @pl.when(is_first)
        def _():
            before_ref[...] = outer_ref[...]
            after_ref[...] = inner_ref[...]

        @pl.when(jnp.logical_not(is_first))
        def _():
            before_ref[...] = inner_ref[...]
            after_ref[...] = outer_ref[...]

    return call(kernel, [(inner.shape, inner.dtype)] * 2, inner, outer)


def line_slots(squares):
    def slots(z):
        slot, first, count = 0, 0, 2
        while first < squares:
            for corner in range(4):
                for k in range(count):
                    yield slot, square_of(z, first + k, squares), corner // 2, corner % 2
                    slot += 1
            first, count = first + count, first + count

    return slots


def assemble_conv(pieces, taps):
    squares = lax.axis_size("ctx") // 8
    width = pieces[0].shape[-1]
    rows = pieces[0].shape[-2] // taps

    def kernel(*refs):
        out = refs[-1]
        core, x, y, z = place()
        for dc in range(2):
            for slot, source, dy, dx in line_slots(squares)(z):
                for t in range(taps):
                    part = refs[dc][slot, t * rows : (t + 1) * rows]
                    out[t, source, y ^ dy, x ^ dx, core ^ dc] = part

    out = call(kernel, [((taps, squares, 2, 2, 2, rows, width), pieces[0].dtype)], *pieces)[0]
    return out.reshape(taps, squares * 8 * rows, width)


def assemble_down(pieces, rows):
    squares = lax.axis_size("ctx") // 8
    width = pieces[0].shape[-1]

    def kernel(own_ref, other_ref, out, wide):
        core, x, y, z = place()
        is_first = core == 0
        for slot, source, dy, dx in line_slots(squares)(z):
            mine = own_ref[slot, :rows].astype(jnp.float32)
            theirs = other_ref[slot, :rows].astype(jnp.float32)
            wide[:rows] = jnp.where(is_first, mine, theirs)
            wide[rows:] = jnp.where(is_first, theirs, mine)
            out[source, y ^ dy, x ^ dx] = wide[...].astype(jnp.bfloat16)

    out = call(
        kernel,
        [((squares, 2, 2, 2 * rows, width), pieces[0].dtype)],
        *pieces,
        scratch=[pltpu.VMEM((2 * rows, width), jnp.float32)],
    )[0]
    return out.reshape(squares * 8 * rows, width)


def assemble_up(pieces, rows, width):
    squares = lax.axis_size("ctx") // 8

    def kernel(*refs):
        out = refs[-1]
        core, x, y, z = place()
        for piece, index, source, dy, dx, dc in up_slots(squares)(z):
            out[source, y ^ dy, x ^ dx, core ^ dc] = refs[piece][index]

    out = call(kernel, [((squares, 2, 2, 2, rows, width), pieces[0].dtype)], *pieces)[0]
    return out.reshape(squares * 8 * rows, width)


def line_masks(squares):
    return [8 << i for i in reversed(range(squares.bit_length() - 1))]


def square_of(z, slot, squares):
    for i, mask in enumerate(line_masks(squares)):
        if slot >> i & 1:
            z = z ^ (mask // 8)
    return z


def up_slots(squares):
    def slots(z):
        for core in range(2):
            for k in range(squares):
                for corner in range(4):
                    source = square_of(z, k, squares)
                    yield core, (4 * k + corner,), source, corner // 2, corner % 2, core

    return slots


def all_after(values, others):
    count = len(values)
    return lax.optimization_barrier((*values, *others))[:count]


def load(*arrays):
    count = len(arrays)

    def kernel(*refs):
        ins, outs, sem = refs[:count], refs[count:-1], refs[-1]
        copies = [pltpu.make_async_copy(i, o, sem.at[at]) for at, (i, o) in enumerate(zip(ins, outs))]
        for copy in copies:
            copy.start()
        for copy in copies:
            copy.wait()

    return pl.pallas_call(
        kernel,
        out_shape=[jax.ShapeDtypeStruct(a.shape, a.dtype) for a in arrays],
        in_specs=[pl.BlockSpec(memory_space=pltpu.HBM)] * count,
        out_specs=[VMEM] * count,
        scratch_shapes=[pltpu.SemaphoreType.DMA((count,))],
        compiler_params=PARAMS,
        cost_estimate=pl.CostEstimate(flops=1, bytes_accessed=1, transcendentals=0),
    )(*arrays)


def gather(conv, up, down, tokens, cotangent, prepared):
    first, *rest = line_masks(lax.axis_size("ctx") // 8)
    width = conv.shape[-1]
    rows = conv.shape[0] * conv.shape[1]
    filler = jnp.zeros((-(rows + down.shape[0]) % 16, width), conv.dtype)
    both = jnp.concatenate([conv.reshape(rows, width), down, filler])
    inner, outer = neighbours(tokens, cotangent)
    new = swap(both, first)
    up_new = [swap(up, mask) for mask in (2, 4, 6)]
    (up,) = load(up)
    new, outer, both, *up_new = all_after((new, outer, both, *up_new), ())
    part = held = stack([both, new])
    up_held = stack([up] + up_new)
    parts = []
    for mask, next_mask in zip([first] + rest, rest + [None]):
        around = [swap(part, 2), swap(part, 4), swap(part, 6)]
        received = swap(up_held, mask)
        other = swap(inner, 1) if next_mask is None else swap(held, next_mask)
        part, held, up_held, received, other, *around = all_after(
            (part, held, up_held, received, other, *around), ()
        )
        up_held = join(up_held, received)
        parts += [part, *around]
        if next_mask is not None:
            held, part = join(held, other), other
    all_conv, all_down = join_rows(parts, rows)
    extra = prepared(tokens, cotangent, *in_order(other, outer))
    return [(piece, swap(piece, 1)) for piece in (all_conv, up_held, all_down)], extra


def core_rows(rows):
    start = (rows // 2 - 2) // 8 * 8
    return start, rows - start


def relative_blocks(total):
    squares = lax.axis_size("ctx") // 8
    rows, width = total.shape[0] // (4 * squares), total.shape[1]
    start, held = core_rows(rows)
    blocks = total.reshape(squares, 2, 2, rows, width)

    def kernel(blocks_ref, keep_ref, send_ref):
        core, x, y, z = place()
        keep = pl.ds(pl.multiple_of(core * start, 8), held)
        send = pl.ds(pl.multiple_of((1 - core) * start, 8), held)
        for k in range(squares):
            for dy in range(2):
                for dx in range(2):
                    keep_ref[k, dy, dx] = blocks_ref[z ^ k, y ^ dy, x ^ dx, keep, :]
                    send_ref[k, dy, dx] = blocks_ref[z ^ k, y ^ dy, x ^ dx, send, :].astype(jnp.bfloat16)

    shape = (squares, 2, 2, held, width)
    return call(kernel, [(shape, jnp.float32), (shape, jnp.bfloat16)], blocks)


def chip_sums(keep, received):
    squares, _, _, held, width = keep.shape

    def kernel(keep_ref, received_ref, own_ref, x_ref, y_ref, far_ref):
        for k in range(squares):
            for corner, ref in enumerate((own_ref, x_ref, y_ref, far_ref)):
                at = (k, corner // 2, corner % 2)
                ref[k] = (keep_ref[at] + received_ref[at].astype(jnp.float32)).astype(ref.dtype)

    shape = (squares, held, width)
    return call(
        kernel, [(shape, jnp.float32)] + [(shape, jnp.bfloat16)] * 3, keep, received
    )


def line_messages(own, received, gain, each):
    squares, held, width = own.shape

    def kernel(own_ref, x_ref, y_ref, far_ref, gain_ref, sum_ref, *message_refs):
        gain = gain_ref[...]
        high = gain.astype(jnp.bfloat16).astype(jnp.float32)
        row = lax.broadcasted_iota(jnp.int32, (held, width), 0)
        row = row - jnp.where(lax.axis_index("ctx") % 2 == 0, each, 0)
        for k in range(squares):
            total = own_ref[k]
            for ref in (x_ref, y_ref, far_ref):
                total = total + ref[k].astype(jnp.float32)
            if k == 0:
                sum_ref[...] = total
            else:
                total = jnp.where(row == 0, high, jnp.where(row == 1, gain - high, total))
                message_refs[k - 1][...] = total.astype(jnp.bfloat16)

    return call(
        kernel,
        [((held, width), jnp.float32)] + [((held, width), jnp.bfloat16)] * (squares - 1),
        own,
        *received,
        gain,
    )


def finish(own, gain, received, each, factor):
    held, width = own.shape

    def kernel(own_ref, gain_ref, *refs):
        received_refs, (down_ref, out_ref) = refs[:-2], refs[-2:]
        is_first = lax.axis_index("ctx") % 2 == 0
        total, gain = own_ref[...], gain_ref[...]
        for ref in received_refs:
            terms = ref[...].astype(jnp.float32)
            total = total + terms
            high = jnp.where(is_first, terms[each : each + 1], terms[:1])
            gain = gain + (high + jnp.where(is_first, terms[each + 1 : each + 2], terms[1:2]))
        down_ref[...] = jnp.where(is_first, total[:each], total[held - each :]) * factor
        out_ref[...] = (gain * factor).reshape(width)

    return call(
        kernel,
        [((each, width), jnp.float32), ((width,), jnp.float32)],
        own,
        gain,
        *received,
    )


def body(tokens, cotangent, norm_gain, conv_weight, up_weight, down_weight, contig_first_bins):
    seqs, bins, width = tokens.shape
    ctx_count = lax.axis_size("ctx")
    data_count = lax.axis_size("dp")
    squares = ctx_count // 8
    gain = norm_gain.reshape(1, width)


    def prepared(tokens, cotangent, before, after_):
        normed = prepare(before, tokens, after_, gain, contig_first_bins)
        return (tokens, cotangent, before, after_, *normed)

    (conv_pieces, up_pieces, down_pieces), extra = gather(
        conv_weight, up_weight, down_weight, tokens, cotangent, prepared
    )
    tokens, cotangent, before, after_, taps, scaled, inverse = extra
    conv = assemble_conv(conv_pieces, conv_weight.shape[0])
    mixed = convolve(taps, before, tokens, after_, conv)
    up = assemble_up(up_pieces, *up_weight.shape)
    pre, share, hidden, total = expand(mixed, up, cotangent)
    slope = slopes(mixed, up, pre, share)
    keep, send = relative_blocks(total)
    down = assemble_down(down_pieces, down_weight.shape[0])
    own_line, *others = chip_sums(keep, after(swap(send, 1), slope))
    received = [swap(v, mask) for v, mask in zip(others, (2, 4, 6))]
    input_grad, gain_term = backward(
        before,
        cotangent,
        after_,
        slope,
        down,
        up,
        conv,
        scaled,
        inverse,
        gain,
        contig_first_bins,
    )
    output = project(mixed, hidden, down)
    for mask in (1, 2, 4):
        if mask == 4:
            gain_term = after(gain_term, output)
        gain_term = gain_term + swap(gain_term, mask)
    factor = float(ctx_count * data_count * bins * seqs) ** (-0.5)
    each = total.shape[0] // ctx_count
    own_sum, *messages = line_messages(own_line, received, gain_term, each)
    arrived = [swap(message, 8 * (k + 1)) for k, message in enumerate(messages)]
    down_part, gain_all = finish(own_sum, gain_term, arrived, each, factor)
    gain_part = gain_all
    if data_count > 1:
        width_part = width // data_count
        down_part = lax.psum_scatter(down_part, "dp", scatter_dimension=1, tiled=True)
        gain_part = lax.psum(gain_part, "dp")
        at = lax.axis_index("dp") * width_part
        gain_part = lax.dynamic_slice_in_dim(gain_part, at, width_part)
    return output, input_grad, down_part, gain_part


def solution(mesh):
    placed = (
        P("dp", "ctx", None),
        P("dp", "ctx", None),
        P(),
        P(None, "ctx", None),
        P("ctx", None),
        P("ctx", None),
        P(),
    )
    return jax.shard_map(
        body,
        mesh=mesh,
        in_specs=placed,
        out_specs=(P("dp", "ctx", None), P("dp", "ctx", None), P("ctx", "dp"), P("dp")),
        check_vma=False,
    )
```

```python
import jax
import jax.numpy as jnp
from jax import lax
from jax.experimental import pallas as pl
from jax.experimental.pallas import tpu as pltpu
from jax.sharding import PartitionSpec as P

DILATION_BINS = 64


root_half = 0.7071067811865476
inv_root_two_pi = 0.3989422804014327


def swap(value, mask):
    devices = lax.axis_size("ctx")
    return lax.ppermute(value, "ctx", [(i, i ^ mask) for i in range(devices)])


def place():
    me = lax.axis_index("ctx")
    return me % 2, (me // 2) % 2, (me // 4) % 2, me // 8


def after(value, *others):
    return lax.optimization_barrier((value,) + others)[0]


VMEM = pl.BlockSpec(memory_space=pltpu.VMEM)
FIRST, SECOND, THIRD, LAST = 5000000000, 2000000000, 4500000000, 40000000000
PARAMS = pltpu.CompilerParams(vmem_limit_bytes=20 * 1024 * 1024)

SMEM = pl.BlockSpec(memory_space=pltpu.SMEM)


def call(kernel, outs, *args, smem=(), scratch=(), cost=1):
    shapes = [jax.ShapeDtypeStruct(shape, dtype) for shape, dtype in outs]
    return pl.pallas_call(
        kernel,
        out_shape=shapes,
        in_specs=[SMEM if i in smem else VMEM for i in range(len(args))],
        out_specs=[VMEM] * len(shapes),
        scratch_shapes=list(scratch),
        compiler_params=PARAMS,
        cost_estimate=pl.CostEstimate(flops=cost, bytes_accessed=1, transcendentals=0),
    )(*args)


def segment_of(position, starts_ref):
    segment = jnp.zeros_like(position)
    for i in range(starts_ref.shape[0]):
        segment = segment + jnp.where(position >= starts_ref[i], 1, 0)
    return segment


def masks_at(first, rows, starts_ref, overall):
    position = first + lax.broadcasted_iota(jnp.int32, (rows, 1), 0)
    segment = segment_of(position, starts_ref)
    left = (position >= DILATION_BINS) & (segment_of(position - DILATION_BINS, starts_ref) == segment)
    right = (position + DILATION_BINS < overall) & (
        segment_of(position + DILATION_BINS, starts_ref) == segment
    )
    return left, right


def column_blocks(width):
    step = 384 if width % 384 == 0 else width
    return [slice(at, at + step) for at in range(0, width, step)]


def prepare(before, tokens, after_, gain, starts):
    seqs, bins, width = tokens.shape
    reach = DILATION_BINS
    overall = bins * lax.axis_size("ctx")

    def kernel(before_ref, tokens_ref, after_ref, gain_ref, starts_ref, taps_ref, scaled_ref, inverse_ref):
        first = lax.axis_index("ctx") * bins - reach
        left, right = masks_at(first, bins + 2 * reach, starts_ref, overall)
        for s in range(seqs):
            parts = []
            for ref in (before_ref, tokens_ref, after_ref):
                value = (tokens_ref[s] if ref is tokens_ref else ref[s, : 2 * reach]).astype(jnp.float32)
                inverse = lax.rsqrt(jnp.mean(value * value, axis=1, keepdims=True) + 1e-05)
                scaled = value * inverse
                if ref is tokens_ref:
                    scaled_ref[s] = scaled
                    inverse_ref[s] = inverse
                parts.append(scaled * gain_ref[...])
            normed = jnp.concatenate(parts, axis=0)
            rows = bins + 2 * reach
            taps_ref[s, :, :width] = jnp.where(left, normed[:rows], 0.0).astype(jnp.bfloat16)
            taps_ref[s, :, width : 2 * width] = normed[reach : reach + rows].astype(jnp.bfloat16)
            taps_ref[s, :, 2 * width :] = jnp.where(right, normed[2 * reach :], 0.0).astype(
                jnp.bfloat16
            )

    return call(
        kernel,
        [
            ((seqs, bins + 2 * reach, 3 * width), jnp.bfloat16),
            ((seqs, bins, width), jnp.float32),
            ((seqs, bins, 1), jnp.float32),
        ],
        before,
        tokens,
        after_,
        gain,
        starts,
        smem=(4,),
    )


def convolve(taps, tokens, conv):
    seqs, bins, width = tokens.shape
    reach = DILATION_BINS

    def kernel(taps_ref, tokens_ref, conv_ref, mixed_ref):
        for s in range(seqs):
            for at in column_blocks(width):
                mixed_ref[s, :, at] = tokens_ref[s, :, at].astype(jnp.float32) + jnp.dot(
                    taps_ref[s, reach : reach + bins],
                    conv_ref[:, at],
                    preferred_element_type=jnp.float32,
                )

    return call(
        kernel, [((seqs, bins, width), jnp.float32)], taps, tokens, conv.reshape(-1, width)
    )[0]


def expand(mixed, up, cotangent):
    seqs, bins, width = cotangent.shape
    hidden_width = up.shape[1]

    def kernel(mixed_ref, up_ref, cotangent_ref, pre_ref, share_ref, hidden_ref, total_ref):
        for s in range(seqs):
            low = mixed_ref[s].astype(jnp.bfloat16)
            for at in column_blocks(hidden_width):
                pre = jnp.dot(low, up_ref[:, at], preferred_element_type=jnp.float32)
                share = 0.5 * (1.0 + lax.erf(pre * root_half))
                hidden = (pre * share).astype(jnp.bfloat16)
                pre_ref[s, :, at] = pre
                share_ref[s, :, at] = share
                hidden_ref[s, :, at] = hidden
                term = lax.dot_general(
                    hidden,
                    cotangent_ref[s],
                    (((0,), (0,)), ((), ())),
                    preferred_element_type=jnp.float32,
                )
                if s == 0:
                    total_ref[at, :] = term
                else:
                    total_ref[at, :] += term

    return call(
        kernel,
        [
            ((seqs, bins, hidden_width), jnp.float32),
            ((seqs, bins, hidden_width), jnp.float32),
            ((seqs, bins, hidden_width), jnp.bfloat16),
            ((hidden_width, width), jnp.float32),
        ],
        mixed,
        up,
        cotangent,
    )


def slopes(taps, before, after_, conv, up, pre, share):
    seqs, bins, hidden_width = pre.shape
    width = before.shape[2]
    reach = DILATION_BINS
    rows = bins + 2 * reach

    def bell(value):
        return value * jnp.exp(-0.5 * value * value) * inv_root_two_pi

    def kernel(taps_ref, before_ref, after_ref, conv_ref, up_ref, pre_ref, share_ref, slope_ref, mixed):
        for s in range(seqs):
            edges = jnp.concatenate([taps_ref[s, :reach], taps_ref[s, reach + bins :]], axis=0)
            tokens = jnp.concatenate([before_ref[s, reach : 2 * reach], after_ref[s, :reach]], axis=0)
            for at in column_blocks(width):
                mixed[:, at] = (
                    tokens[:, at].astype(jnp.float32)
                    + jnp.dot(edges, conv_ref[:, at], preferred_element_type=jnp.float32)
                ).astype(jnp.bfloat16)
            for at in column_blocks(hidden_width):
                edge = jnp.dot(mixed[...], up_ref[:, at], preferred_element_type=jnp.float32)
                slope = 0.5 * (1.0 + lax.erf(edge * root_half)) + bell(edge)
                slope_ref[s, :reach, at] = slope[:reach]
                slope_ref[s, reach : reach + bins, at] = share_ref[s, :, at] + bell(pre_ref[s, :, at])
                slope_ref[s, reach + bins :, at] = slope[reach:]

    return call(
        kernel,
        [((seqs, rows, hidden_width), jnp.float32)],
        taps,
        before,
        after_,
        conv.reshape(-1, width),
        up,
        pre,
        share,
        scratch=[pltpu.VMEM((2 * reach, width), jnp.bfloat16)],
    )[0]


def backward(before, cotangent, after_, slope, down, up, conv, scaled, starts):
    seqs, bins, width = cotangent.shape
    hidden_width = up.shape[1]
    reach = DILATION_BINS
    rows = bins + 2 * reach
    overall = bins * lax.axis_size("ctx")
    by_rows = (((1,), (1,)), ((), ()))

    def kernel(
        before_ref,
        cotangent_ref,
        after_ref,
        slope_ref,
        down_ref,
        up_ref,
        conv_ref,
        scaled_ref,
        starts_ref,
        mixed_grad_ref,
        normed_grad_ref,
        gain_term_ref,
        pre_grad,
        mixed_grad,
    ):
        first = lax.axis_index("ctx") * bins
        left, right = masks_at(first, bins, starts_ref, overall)
        for s in range(seqs):
            cot = jnp.concatenate(
                [before_ref[s, 2 * reach :], cotangent_ref[s], after_ref[s, 2 * reach :]], axis=0
            )
            for at in column_blocks(hidden_width):
                hidden_grad = lax.dot_general(
                    cot, down_ref[at, :], by_rows, preferred_element_type=jnp.float32
                )
                pre_grad[:, at] = (hidden_grad * slope_ref[s, :, at]).astype(jnp.bfloat16)
            for at in column_blocks(width):
                mixed_grad[:, at] = cot[:, at].astype(jnp.float32) + lax.dot_general(
                    pre_grad[...], up_ref[at, :], by_rows, preferred_element_type=jnp.float32
                )
            following = jnp.where(right, mixed_grad[2 * reach :, :], 0.0).astype(jnp.bfloat16)
            center = mixed_grad[reach : reach + bins, :].astype(jnp.bfloat16)
            preceding = jnp.where(left, mixed_grad[:bins, :], 0.0).astype(jnp.bfloat16)
            mixed_grad_ref[s] = mixed_grad[reach : reach + bins, :]
            for at in column_blocks(width):
                normed_grad = (
                    lax.dot_general(following, conv_ref[0, at, :], by_rows, preferred_element_type=jnp.float32)
                    + lax.dot_general(center, conv_ref[1, at, :], by_rows, preferred_element_type=jnp.float32)
                    + lax.dot_general(preceding, conv_ref[2, at, :], by_rows, preferred_element_type=jnp.float32)
                )
                normed_grad_ref[s, :, at] = normed_grad
                term = jnp.sum(normed_grad * scaled_ref[s, :, at], axis=0, keepdims=True)
                if s == 0:
                    gain_term_ref[:, at] = term
                else:
                    gain_term_ref[:, at] += term

    return call(
        kernel,
        [
            ((seqs, bins, width), jnp.float32),
            ((seqs, bins, width), jnp.float32),
            ((1, width), jnp.float32),
        ],
        before,
        cotangent,
        after_,
        slope,
        down,
        up,
        conv,
        scaled,
        starts,
        smem=(8,),
        scratch=[
            pltpu.VMEM((rows, hidden_width), jnp.bfloat16),
            pltpu.VMEM((rows, width), jnp.float32),
        ],
    )


def finish_rows(mixed, hidden, down, mixed_grad, normed_grad, scaled, inverse, gain):
    seqs, bins, _ = hidden.shape
    width = down.shape[1]

    def kernel(
        mixed_ref,
        hidden_ref,
        down_ref,
        mixed_grad_ref,
        normed_grad_ref,
        scaled_ref,
        inverse_ref,
        gain_ref,
        out_ref,
        grad_ref,
    ):
        for s in range(seqs):
            scaled = scaled_ref[s]
            scaled_grad = normed_grad_ref[s] * gain_ref[...]
            inner = jnp.mean(scaled_grad * scaled, axis=1, keepdims=True)
            grad_ref[s] = (
                mixed_grad_ref[s] + inverse_ref[s] * (scaled_grad - scaled * inner)
            ).astype(jnp.bfloat16)
            for at in column_blocks(width):
                out_ref[s, :, at] = (
                    mixed_ref[s, :, at]
                    + jnp.dot(hidden_ref[s], down_ref[:, at], preferred_element_type=jnp.float32)
                ).astype(jnp.bfloat16)

    return call(
        kernel,
        [((seqs, bins, width), jnp.bfloat16)] * 2,
        mixed,
        hidden,
        down,
        mixed_grad,
        normed_grad,
        scaled,
        inverse,
        gain,
    )


def stack(pieces, cost=1):
    def kernel(*refs):
        for i in range(len(pieces)):
            refs[-1][i] = refs[i][...]

    shape = (len(pieces),) + pieces[0].shape
    return call(kernel, [(shape, pieces[0].dtype)], *pieces, cost=cost)[0]


def join(*pieces, cost=1):
    ends = [sum(piece.shape[0] for piece in pieces[: i + 1]) for i in range(len(pieces))]

    def kernel(*refs):
        for ref, end in zip(refs[:-1], ends):
            refs[-1][end - ref.shape[0] : end] = ref[...]

    shape = (ends[-1],) + pieces[0].shape[1:]
    return call(kernel, [(shape, pieces[0].dtype)], *pieces, cost=cost)[0]


def join_rows(pieces, rows, cost=1):
    ends = [sum(stop - start for _, start, stop in pieces[: i + 1]) for i in range(len(pieces))]
    held, width = pieces[0][0].shape[1:]

    def kernel(*refs):
        for ref, (_, start, stop), end in zip(refs[:-2], pieces, ends):
            at = slice(end - (stop - start), end)
            refs[-2][at] = ref[start:stop, :rows]
            refs[-1][at] = ref[start:stop, rows:]

    shapes = [(ends[-1], rows, width), (ends[-1], held - rows, width)]
    arrays = [piece[0] for piece in pieces]
    return call(kernel, [(shape, arrays[0].dtype) for shape in shapes], *arrays, cost=cost)


def join_parts(*pieces):
    ends = [sum(stop - start for _, start, stop in pieces[: i + 1]) for i in range(len(pieces))]

    def kernel(*refs):
        for ref, (_, start, stop), end in zip(refs[:-1], pieces, ends):
            refs[-1][end - (stop - start) : end] = ref[start:stop]

    shape = (ends[-1],) + pieces[0][0].shape[1:]
    return call(kernel, [(shape, pieces[0][0].dtype)], *[p[0] for p in pieces])[0]


def neighbours(tokens, cotangent):
    devices = lax.axis_size("ctx")
    pairs = [(i, i + 1) for i in range(1, devices - 1, 2)]
    pairs += [(j, i) for i, j in pairs]
    far, near = 2 * DILATION_BINS, DILATION_BINS
    seqs, bins, width = tokens.shape

    def cut(tokens_ref, cotangent_ref, last_ref, leading_ref):
        last_ref[:, :far] = tokens_ref[:, bins - far :]
        last_ref[:, far:] = cotangent_ref[:, bins - near :]
        leading_ref[:, :far] = tokens_ref[:, :far]
        leading_ref[:, far:] = cotangent_ref[:, :near]

    def kernel(tokens_ref, cotangent_ref, inner_ref, outer_ref):
        is_first = lax.axis_index("ctx") % 2 == 0

        @pl.when(is_first)
        def _():
            cut(tokens_ref, cotangent_ref, inner_ref, outer_ref)

        @pl.when(jnp.logical_not(is_first))
        def _():
            cut(tokens_ref, cotangent_ref, outer_ref, inner_ref)

    edge = ((seqs, far + near, width), tokens.dtype)
    inner, outer = call(kernel, [edge, edge], tokens, cotangent)
    return inner, lax.ppermute(outer, "ctx", pairs)


def in_order(inner, outer):
    def kernel(inner_ref, outer_ref, before_ref, after_ref):
        is_first = lax.axis_index("ctx") % 2 == 0

        @pl.when(is_first)
        def _():
            before_ref[...] = outer_ref[...]
            after_ref[...] = inner_ref[...]

        @pl.when(jnp.logical_not(is_first))
        def _():
            before_ref[...] = inner_ref[...]
            after_ref[...] = outer_ref[...]

    return call(kernel, [(inner.shape, inner.dtype)] * 2, inner, outer)


def line_slots(squares):
    def slots(z):
        slot, first, count = 0, 0, 2
        while first < squares:
            for corner in range(4):
                last = corner == 3 and first + count == squares
                for k in range(count):
                    source = square_of(z, first + k, squares)
                    yield int(last), k if last else slot, source, corner // 2, corner % 2
                    slot += 1
            first, count = first + count, first + count

    return slots


def assemble_conv(pieces, taps):
    squares = lax.axis_size("ctx") // 8
    width = pieces[0].shape[-1]
    rows = pieces[0].shape[-2] // taps

    def kernel(*refs):
        out = refs[-1]
        core, x, y, z = place()
        for dc in range(2):
            for last, slot, source, dy, dx in line_slots(squares)(z):
                for t in range(taps):
                    part = refs[2 * last + dc][slot, t * rows : (t + 1) * rows]
                    out[t, source, y ^ dy, x ^ dx, core ^ dc] = part

    out = call(kernel, [((taps, squares, 2, 2, 2, rows, width), pieces[0].dtype)], *pieces)[0]
    return out.reshape(taps, squares * 8 * rows, width)


def assemble_down(pieces, rows):
    squares = lax.axis_size("ctx") // 8
    width = pieces[0].shape[-1]

    def kernel(*refs):
        out, wide = refs[-2:]
        core, x, y, z = place()
        is_first = core == 0
        for last, slot, source, dy, dx in line_slots(squares)(z):
            mine = refs[2 * last][slot, :rows].astype(jnp.float32)
            theirs = refs[2 * last + 1][slot, :rows].astype(jnp.float32)
            wide[:rows] = jnp.where(is_first, mine, theirs)
            wide[rows:] = jnp.where(is_first, theirs, mine)
            out[source, y ^ dy, x ^ dx] = wide[...].astype(jnp.bfloat16)

    out = call(
        kernel,
        [((squares, 2, 2, 2 * rows, width), pieces[0].dtype)],
        *pieces,
        scratch=[pltpu.VMEM((2 * rows, width), jnp.float32)],
    )[0]
    return out.reshape(squares * 8 * rows, width)


def assemble_up(pieces, rows, width):
    squares = lax.axis_size("ctx") // 8

    def kernel(*refs):
        out = refs[-1]
        core, x, y, z = place()
        for piece, index, source, dy, dx, dc in up_slots(squares)(z):
            out[source, y ^ dy, x ^ dx, core ^ dc] = refs[piece][index]

    out = call(kernel, [((squares, 2, 2, 2, rows, width), pieces[0].dtype)], *pieces)[0]
    return out.reshape(squares * 8 * rows, width)


def line_masks(squares):
    return [8 << i for i in reversed(range(squares.bit_length() - 1))]


def square_of(z, slot, squares):
    for i, mask in enumerate(line_masks(squares)):
        if slot >> i & 1:
            z = z ^ (mask // 8)
    return z


def up_slots(squares):
    def slots(z):
        for core in range(2):
            for k in range(squares):
                for corner in range(4):
                    source = square_of(z, k, squares)
                    yield core, (4 * k + corner,), source, corner // 2, corner % 2, core

    return slots


def all_after(values, others):
    count = len(values)
    return lax.optimization_barrier((*values, *others))[:count]


def load(*arrays):
    count = len(arrays)

    def kernel(*refs):
        ins, outs, sem = refs[:count], refs[count:-1], refs[-1]
        copies = [pltpu.make_async_copy(i, o, sem.at[at]) for at, (i, o) in enumerate(zip(ins, outs))]
        for copy in copies:
            copy.start()
        for copy in copies:
            copy.wait()

    return pl.pallas_call(
        kernel,
        out_shape=[jax.ShapeDtypeStruct(a.shape, a.dtype) for a in arrays],
        in_specs=[pl.BlockSpec(memory_space=pltpu.HBM)] * count,
        out_specs=[VMEM] * count,
        scratch_shapes=[pltpu.SemaphoreType.DMA((count,))],
        compiler_params=PARAMS,
        cost_estimate=pl.CostEstimate(flops=1, bytes_accessed=1, transcendentals=0),
    )(*arrays)


def gather(conv, up, down, tokens, cotangent, prepared):
    first, *rest = line_masks(lax.axis_size("ctx") // 8)
    width = conv.shape[-1]
    rows = conv.shape[0] * conv.shape[1]
    filler = jnp.zeros((-(rows + down.shape[0]) % 16, width), conv.dtype)
    both = jnp.concatenate([conv.reshape(rows, width), down, filler])
    new = swap(both, first)
    up_new = [swap(up, mask) for mask in (2, 4, 6)]
    inner, outer = neighbours(*all_after((tokens, cotangent), (up_new[0],)))
    (up,) = load(up)
    new, both, *up_new = all_after((new, both, *up_new), ())
    part = held = stack([both, new], cost=FIRST)
    up_held = stack([up] + up_new, cost=SECOND)
    pieces, late = [], None
    for mask, next_mask in zip([first] + rest, rest + [None]):
        count = part.shape[0]
        if late is None:
            to_x, to_y = part, part
        else:
            old, old_x, old_y = late
            to_x = join_parts((part, 0, count), (old_y, old // 2, old))
            to_y = join_parts((part, 0, count), (old_x, 0, old // 2))
        by_x, by_y, received = swap(to_x, 2), swap(to_y, 4), swap(up_held, mask)
        other = swap(inner, 1) if next_mask is None else swap(held, next_mask)
        up_held = join(up_held, received)
        if next_mask is None:
            outer = stack([outer], cost=THIRD)
        part, held, up_held, by_x, by_y, other, outer = all_after(
            (part, held, up_held, by_x, by_y, other, outer), ()
        ) if next_mask is None else (*all_after((part, held, up_held, by_x, by_y, other), ()), outer)
        if late is not None:
            pieces += [(by_y, count, count + old // 2), (by_x, count, count + old - old // 2)]
        pieces += [(part, 0, count), (by_x, 0, count), (by_y, 0, count)]
        late = (count, by_x, by_y)
        if next_mask is not None:
            held, part = join(held, other), other
    half = count // 2
    far_first = swap(join_parts((by_x, 0, half)), 4)
    far_second = swap(join_parts((by_y, half, count)), 2)
    extra = prepared(tokens, cotangent, *in_order(other, outer[0]))
    far_first = after(far_first, extra[4])
    most = join_rows(pieces, rows)
    last = join_rows([(far_first, 0, half), (far_second, 0, count - half)], rows, cost=LAST)
    pieces = [(most[0], last[0]), (up_held,), (most[1], last[1])]
    return [[both for p in piece for both in (p, swap(p, 1))] for piece in pieces], extra


def core_rows(rows):
    start = (rows // 2 - 2) // 8 * 8
    return start, rows - start


def relative_blocks(total):
    squares = lax.axis_size("ctx") // 8
    rows, width = total.shape[0] // (4 * squares), total.shape[1]
    start, held = core_rows(rows)
    blocks = total.reshape(squares, 2, 2, rows, width)

    def kernel(blocks_ref, keep_ref, send_ref):
        core, x, y, z = place()
        keep = pl.ds(pl.multiple_of(core * start, 8), held)
        send = pl.ds(pl.multiple_of((1 - core) * start, 8), held)
        for k in range(squares):
            for dy in range(2):
                for dx in range(2):
                    keep_ref[k, dy, dx] = blocks_ref[z ^ k, y ^ dy, x ^ dx, keep, :]
                    send_ref[k, dy, dx] = blocks_ref[z ^ k, y ^ dy, x ^ dx, send, :].astype(jnp.bfloat16)

    shape = (squares, 2, 2, held, width)
    return call(kernel, [(shape, jnp.float32), (shape, jnp.bfloat16)], blocks)


def chip_sums(keep, received):
    squares, _, _, held, width = keep.shape

    def kernel(keep_ref, received_ref, own_ref, x_ref, y_ref, far_ref):
        for k in range(squares):
            for corner, ref in enumerate((own_ref, x_ref, y_ref, far_ref)):
                at = (k, corner // 2, corner % 2)
                ref[k] = (keep_ref[at] + received_ref[at].astype(jnp.float32)).astype(ref.dtype)

    shape = (squares, held, width)
    return call(
        kernel, [(shape, jnp.float32)] + [(shape, jnp.bfloat16)] * 3, keep, received
    )


def line_messages(own, received, gain, each):
    squares, held, width = own.shape

    def kernel(own_ref, x_ref, y_ref, far_ref, gain_ref, sum_ref, *message_refs):
        gain = gain_ref[...]
        high = gain.astype(jnp.bfloat16).astype(jnp.float32)
        row = lax.broadcasted_iota(jnp.int32, (held, width), 0)
        row = row - jnp.where(lax.axis_index("ctx") % 2 == 0, each, 0)
        for k in range(squares):
            total = own_ref[k]
            for ref in (x_ref, y_ref, far_ref):
                total = total + ref[k].astype(jnp.float32)
            if k == 0:
                sum_ref[...] = total
            else:
                total = jnp.where(row == 0, high, jnp.where(row == 1, gain - high, total))
                message_refs[k - 1][...] = total.astype(jnp.bfloat16)

    return call(
        kernel,
        [((held, width), jnp.float32)] + [((held, width), jnp.bfloat16)] * (squares - 1),
        own,
        *received,
        gain,
    )


def finish(own, gain, received, each, factor):
    held, width = own.shape

    def kernel(own_ref, gain_ref, *refs):
        received_refs, (down_ref, out_ref) = refs[:-2], refs[-2:]
        is_first = lax.axis_index("ctx") % 2 == 0
        total, gain = own_ref[...], gain_ref[...]
        for ref in received_refs:
            terms = ref[...].astype(jnp.float32)
            total = total + terms
            high = jnp.where(is_first, terms[each : each + 1], terms[:1])
            gain = gain + (high + jnp.where(is_first, terms[each + 1 : each + 2], terms[1:2]))
        down_ref[...] = jnp.where(is_first, total[:each], total[held - each :]) * factor
        out_ref[...] = (gain * factor).reshape(width)

    return call(
        kernel,
        [((each, width), jnp.float32), ((width,), jnp.float32)],
        own,
        gain,
        *received,
    )


def body(tokens, cotangent, norm_gain, conv_weight, up_weight, down_weight, contig_first_bins):
    seqs, bins, width = tokens.shape
    ctx_count = lax.axis_size("ctx")
    data_count = lax.axis_size("dp")
    squares = ctx_count // 8
    gain = norm_gain.reshape(1, width)


    def prepared(tokens, cotangent, before, after_):
        normed = prepare(before, tokens, after_, gain, contig_first_bins)
        return (tokens, cotangent, before, after_, *normed)

    (conv_pieces, up_pieces, down_pieces), extra = gather(
        conv_weight, up_weight, down_weight, tokens, cotangent, prepared
    )
    tokens, cotangent, before, after_, taps, scaled, inverse = extra
    conv = assemble_conv(conv_pieces, conv_weight.shape[0])
    mixed = convolve(taps, tokens, conv)
    up = assemble_up(up_pieces, *up_weight.shape)
    mixed = after(mixed, *down_pieces)
    pre, share, hidden, total = expand(mixed, up, cotangent)
    slope = slopes(taps, before, after_, conv, up, pre, share)
    keep, send = relative_blocks(total)
    down = assemble_down(down_pieces, down_weight.shape[0])
    own_line, *others = chip_sums(keep, after(swap(send, 1), slope, down))
    received = [swap(v, mask) for v, mask in zip(others, (2, 4, 6))]
    mixed_grad, normed_grad, gain_term = backward(
        before, cotangent, after_, slope, down, up, conv, scaled, contig_first_bins
    )
    output, input_grad = finish_rows(
        mixed, hidden, down, mixed_grad, normed_grad, scaled, inverse, gain
    )
    for mask in (1, 2, 4):
        if mask == 4:
            gain_term = after(gain_term, output)
        gain_term = gain_term + swap(gain_term, mask)
    factor = float(ctx_count * data_count * bins * seqs) ** (-0.5)
    each = total.shape[0] // ctx_count
    own_sum, *messages = line_messages(own_line, received, gain_term, each)
    arrived = [swap(message, 8 * (k + 1)) for k, message in enumerate(messages)]
    down_part, gain_all = finish(own_sum, gain_term, arrived, each, factor)
    gain_part = gain_all
    if data_count > 1:
        width_part = width // data_count
        down_part = lax.psum_scatter(down_part, "dp", scatter_dimension=1, tiled=True)
        gain_part = lax.psum(gain_part, "dp")
        at = lax.axis_index("dp") * width_part
        gain_part = lax.dynamic_slice_in_dim(gain_part, at, width_part)
    return output, input_grad, down_part, gain_part


def solution(mesh):
    placed = (
        P("dp", "ctx", None),
        P("dp", "ctx", None),
        P(),
        P(None, "ctx", None),
        P("ctx", None),
        P("ctx", None),
        P(),
    )
    return jax.shard_map(
        body,
        mesh=mesh,
        in_specs=placed,
        out_specs=(P("dp", "ctx", None), P("dp", "ctx", None), P("ctx", "dp"), P("dp")),
        check_vma=False,
    )
```

```python
import jax
import jax.numpy as jnp
from jax import lax
from jax.experimental import pallas as pl
from jax.experimental.pallas import tpu as pltpu
from jax.sharding import PartitionSpec as P

DILATION_BINS = 64


root_half = 0.7071067811865476
inv_root_two_pi = 0.3989422804014327


def swap(value, mask):
    devices = lax.axis_size("ctx")
    return lax.ppermute(value, "ctx", [(i, i ^ mask) for i in range(devices)])


def place():
    me = lax.axis_index("ctx")
    return me % 2, (me // 2) % 2, (me // 4) % 2, me // 8


def after(value, *others):
    return lax.optimization_barrier((value,) + others)[0]


VMEM = pl.BlockSpec(memory_space=pltpu.VMEM)
FIRST, SECOND, THIRD, LAST = 5000000000, 2000000000, 4500000000, 40000000000
PARAMS = pltpu.CompilerParams(vmem_limit_bytes=20 * 1024 * 1024)

SMEM = pl.BlockSpec(memory_space=pltpu.SMEM)


def call(kernel, outs, *args, smem=(), scratch=(), cost=1):
    shapes = [jax.ShapeDtypeStruct(shape, dtype) for shape, dtype in outs]
    return pl.pallas_call(
        kernel,
        out_shape=shapes,
        in_specs=[SMEM if i in smem else VMEM for i in range(len(args))],
        out_specs=[VMEM] * len(shapes),
        scratch_shapes=list(scratch),
        compiler_params=PARAMS,
        cost_estimate=pl.CostEstimate(flops=cost, bytes_accessed=1, transcendentals=0),
    )(*args)


def segment_of(position, starts_ref):
    segment = jnp.zeros_like(position)
    for i in range(starts_ref.shape[0]):
        segment = segment + jnp.where(position >= starts_ref[i], 1, 0)
    return segment


def masks_at(first, rows, starts_ref, overall):
    position = first + lax.broadcasted_iota(jnp.int32, (rows, 1), 0)
    segment = segment_of(position, starts_ref)
    left = (position >= DILATION_BINS) & (segment_of(position - DILATION_BINS, starts_ref) == segment)
    right = (position + DILATION_BINS < overall) & (
        segment_of(position + DILATION_BINS, starts_ref) == segment
    )
    return left, right


def column_blocks(width):
    step = 384 if width % 384 == 0 else width
    return [slice(at, at + step) for at in range(0, width, step)]


def prepare(before, tokens, after_, gain, starts):
    seqs, bins, width = tokens.shape
    reach = DILATION_BINS
    overall = bins * lax.axis_size("ctx")

    def kernel(before_ref, tokens_ref, after_ref, gain_ref, starts_ref, taps_ref, scaled_ref, inverse_ref):
        first = lax.axis_index("ctx") * bins - reach
        left, right = masks_at(first, bins + 2 * reach, starts_ref, overall)
        for s in range(seqs):
            parts = []
            for ref in (before_ref, tokens_ref, after_ref):
                value = (tokens_ref[s] if ref is tokens_ref else ref[s, : 2 * reach]).astype(jnp.float32)
                inverse = lax.rsqrt(jnp.mean(value * value, axis=1, keepdims=True) + 1e-05)
                scaled = value * inverse
                if ref is tokens_ref:
                    scaled_ref[s] = scaled
                    inverse_ref[s] = inverse
                parts.append(scaled * gain_ref[...])
            normed = jnp.concatenate(parts, axis=0)
            rows = bins + 2 * reach
            taps_ref[s, :, :width] = jnp.where(left, normed[:rows], 0.0).astype(jnp.bfloat16)
            taps_ref[s, :, width : 2 * width] = normed[reach : reach + rows].astype(jnp.bfloat16)
            taps_ref[s, :, 2 * width :] = jnp.where(right, normed[2 * reach :], 0.0).astype(
                jnp.bfloat16
            )

    return call(
        kernel,
        [
            ((seqs, bins + 2 * reach, 3 * width), jnp.bfloat16),
            ((seqs, bins, width), jnp.float32),
            ((seqs, bins, 1), jnp.float32),
        ],
        before,
        tokens,
        after_,
        gain,
        starts,
        smem=(4,),
    )


def convolve(taps, tokens, conv):
    seqs, bins, width = tokens.shape
    reach = DILATION_BINS

    def kernel(taps_ref, tokens_ref, conv_ref, mixed_ref):
        for s in range(seqs):
            for at in column_blocks(width):
                mixed_ref[s, :, at] = tokens_ref[s, :, at].astype(jnp.float32) + jnp.dot(
                    taps_ref[s, reach : reach + bins],
                    conv_ref[:, at],
                    preferred_element_type=jnp.float32,
                )

    return call(
        kernel, [((seqs, bins, width), jnp.float32)], taps, tokens, conv.reshape(-1, width)
    )[0]


def expand(mixed, up, cotangent):
    seqs, bins, width = cotangent.shape
    hidden_width = up.shape[1]

    def kernel(mixed_ref, up_ref, cotangent_ref, pre_ref, share_ref, hidden_ref, total_ref):
        for s in range(seqs):
            low = mixed_ref[s].astype(jnp.bfloat16)
            for at in column_blocks(hidden_width):
                pre = jnp.dot(low, up_ref[:, at], preferred_element_type=jnp.float32)
                share = 0.5 * (1.0 + lax.erf(pre * root_half))
                hidden = (pre * share).astype(jnp.bfloat16)
                pre_ref[s, :, at] = pre
                share_ref[s, :, at] = share
                hidden_ref[s, :, at] = hidden
                term = lax.dot_general(
                    hidden,
                    cotangent_ref[s],
                    (((0,), (0,)), ((), ())),
                    preferred_element_type=jnp.float32,
                )
                if s == 0:
                    total_ref[at, :] = term
                else:
                    total_ref[at, :] += term

    return call(
        kernel,
        [
            ((seqs, bins, hidden_width), jnp.float32),
            ((seqs, bins, hidden_width), jnp.float32),
            ((seqs, bins, hidden_width), jnp.bfloat16),
            ((hidden_width, width), jnp.float32),
        ],
        mixed,
        up,
        cotangent,
    )


def slopes(taps, before, after_, conv, up, pre, share):
    seqs, bins, hidden_width = pre.shape
    width = before.shape[2]
    reach = DILATION_BINS
    rows = bins + 2 * reach

    def bell(value):
        return value * jnp.exp(-0.5 * value * value) * inv_root_two_pi

    def kernel(taps_ref, before_ref, after_ref, conv_ref, up_ref, pre_ref, share_ref, slope_ref, mixed):
        for s in range(seqs):
            edges = jnp.concatenate([taps_ref[s, :reach], taps_ref[s, reach + bins :]], axis=0)
            tokens = jnp.concatenate([before_ref[s, reach : 2 * reach], after_ref[s, :reach]], axis=0)
            for at in column_blocks(width):
                mixed[:, at] = (
                    tokens[:, at].astype(jnp.float32)
                    + jnp.dot(edges, conv_ref[:, at], preferred_element_type=jnp.float32)
                ).astype(jnp.bfloat16)
            for at in column_blocks(hidden_width):
                edge = jnp.dot(mixed[...], up_ref[:, at], preferred_element_type=jnp.float32)
                slope = 0.5 * (1.0 + lax.erf(edge * root_half)) + bell(edge)
                slope_ref[s, :reach, at] = slope[:reach]
                slope_ref[s, reach : reach + bins, at] = share_ref[s, :, at] + bell(pre_ref[s, :, at])
                slope_ref[s, reach + bins :, at] = slope[reach:]

    return call(
        kernel,
        [((seqs, rows, hidden_width), jnp.float32)],
        taps,
        before,
        after_,
        conv.reshape(-1, width),
        up,
        pre,
        share,
        scratch=[pltpu.VMEM((2 * reach, width), jnp.bfloat16)],
    )[0]


def backward(before, cotangent, after_, slope, down, up, conv, scaled, starts):
    seqs, bins, width = cotangent.shape
    hidden_width = up.shape[1]
    reach = DILATION_BINS
    rows = bins + 2 * reach
    overall = bins * lax.axis_size("ctx")
    by_rows = (((1,), (1,)), ((), ()))

    def kernel(
        before_ref,
        cotangent_ref,
        after_ref,
        slope_ref,
        down_ref,
        up_ref,
        conv_ref,
        scaled_ref,
        starts_ref,
        mixed_grad_ref,
        normed_grad_ref,
        gain_term_ref,
        pre_grad,
        mixed_grad,
    ):
        first = lax.axis_index("ctx") * bins
        left, right = masks_at(first, bins, starts_ref, overall)
        for s in range(seqs):
            cot = jnp.concatenate(
                [before_ref[s, 2 * reach :], cotangent_ref[s], after_ref[s, 2 * reach :]], axis=0
            )
            for at in column_blocks(hidden_width):
                hidden_grad = lax.dot_general(
                    cot, down_ref[at, :], by_rows, preferred_element_type=jnp.float32
                )
                pre_grad[:, at] = (hidden_grad * slope_ref[s, :, at]).astype(jnp.bfloat16)
            for at in column_blocks(width):
                mixed_grad[:, at] = cot[:, at].astype(jnp.float32) + lax.dot_general(
                    pre_grad[...], up_ref[at, :], by_rows, preferred_element_type=jnp.float32
                )
            following = jnp.where(right, mixed_grad[2 * reach :, :], 0.0).astype(jnp.bfloat16)
            center = mixed_grad[reach : reach + bins, :].astype(jnp.bfloat16)
            preceding = jnp.where(left, mixed_grad[:bins, :], 0.0).astype(jnp.bfloat16)
            mixed_grad_ref[s] = mixed_grad[reach : reach + bins, :]
            for at in column_blocks(width):
                normed_grad = (
                    lax.dot_general(following, conv_ref[0, at, :], by_rows, preferred_element_type=jnp.float32)
                    + lax.dot_general(center, conv_ref[1, at, :], by_rows, preferred_element_type=jnp.float32)
                    + lax.dot_general(preceding, conv_ref[2, at, :], by_rows, preferred_element_type=jnp.float32)
                )
                normed_grad_ref[s, :, at] = normed_grad
                term = jnp.sum(normed_grad * scaled_ref[s, :, at], axis=0, keepdims=True)
                if s == 0:
                    gain_term_ref[:, at] = term
                else:
                    gain_term_ref[:, at] += term

    return call(
        kernel,
        [
            ((seqs, bins, width), jnp.float32),
            ((seqs, bins, width), jnp.float32),
            ((1, width), jnp.float32),
        ],
        before,
        cotangent,
        after_,
        slope,
        down,
        up,
        conv,
        scaled,
        starts,
        smem=(8,),
        scratch=[
            pltpu.VMEM((rows, hidden_width), jnp.bfloat16),
            pltpu.VMEM((rows, width), jnp.float32),
        ],
    )


def finish_rows(mixed, hidden, down, mixed_grad, normed_grad, scaled, inverse, gain):
    seqs, bins, _ = hidden.shape
    width = down.shape[1]

    def kernel(
        mixed_ref,
        hidden_ref,
        down_ref,
        mixed_grad_ref,
        normed_grad_ref,
        scaled_ref,
        inverse_ref,
        gain_ref,
        out_ref,
        grad_ref,
    ):
        for s in range(seqs):
            scaled = scaled_ref[s]
            scaled_grad = normed_grad_ref[s] * gain_ref[...]
            inner = jnp.mean(scaled_grad * scaled, axis=1, keepdims=True)
            grad_ref[s] = (
                mixed_grad_ref[s] + inverse_ref[s] * (scaled_grad - scaled * inner)
            ).astype(jnp.bfloat16)
            for at in column_blocks(width):
                out_ref[s, :, at] = (
                    mixed_ref[s, :, at]
                    + jnp.dot(hidden_ref[s], down_ref[:, at], preferred_element_type=jnp.float32)
                ).astype(jnp.bfloat16)

    return call(
        kernel,
        [((seqs, bins, width), jnp.bfloat16)] * 2,
        mixed,
        hidden,
        down,
        mixed_grad,
        normed_grad,
        scaled,
        inverse,
        gain,
    )


def stack(pieces, cost=1):
    def kernel(*refs):
        for i in range(len(pieces)):
            refs[-1][i] = refs[i][...]

    shape = (len(pieces),) + pieces[0].shape
    return call(kernel, [(shape, pieces[0].dtype)], *pieces, cost=cost)[0]


def join(*pieces, cost=1):
    ends = [sum(piece.shape[0] for piece in pieces[: i + 1]) for i in range(len(pieces))]

    def kernel(*refs):
        for ref, end in zip(refs[:-1], ends):
            refs[-1][end - ref.shape[0] : end] = ref[...]

    shape = (ends[-1],) + pieces[0].shape[1:]
    return call(kernel, [(shape, pieces[0].dtype)], *pieces, cost=cost)[0]


def join_rows(pieces, rows, cost=1):
    ends = [sum(stop - start for _, start, stop in pieces[: i + 1]) for i in range(len(pieces))]
    held, width = pieces[0][0].shape[1:]

    def kernel(*refs):
        for ref, (_, start, stop), end in zip(refs[:-2], pieces, ends):
            at = slice(end - (stop - start), end)
            refs[-2][at] = ref[start:stop, :rows]
            refs[-1][at] = ref[start:stop, rows:]

    shapes = [(ends[-1], rows, width), (ends[-1], held - rows, width)]
    arrays = [piece[0] for piece in pieces]
    return call(kernel, [(shape, arrays[0].dtype) for shape in shapes], *arrays, cost=cost)


def join_parts(*pieces):
    ends = [sum(stop - start for _, start, stop in pieces[: i + 1]) for i in range(len(pieces))]

    def kernel(*refs):
        for ref, (_, start, stop), end in zip(refs[:-1], pieces, ends):
            refs[-1][end - (stop - start) : end] = ref[start:stop]

    shape = (ends[-1],) + pieces[0][0].shape[1:]
    return call(kernel, [(shape, pieces[0][0].dtype)], *[p[0] for p in pieces])[0]


def neighbours(tokens, cotangent):
    devices = lax.axis_size("ctx")
    pairs = [(i, i + 1) for i in range(1, devices - 1, 2)]
    pairs += [(j, i) for i, j in pairs]
    far, near = 2 * DILATION_BINS, DILATION_BINS
    seqs, bins, width = tokens.shape

    def cut(tokens_ref, cotangent_ref, last_ref, leading_ref):
        last_ref[:, :far] = tokens_ref[:, bins - far :]
        last_ref[:, far:] = cotangent_ref[:, bins - near :]
        leading_ref[:, :far] = tokens_ref[:, :far]
        leading_ref[:, far:] = cotangent_ref[:, :near]

    def kernel(tokens_ref, cotangent_ref, inner_ref, outer_ref):
        is_first = lax.axis_index("ctx") % 2 == 0

        @pl.when(is_first)
        def _():
            cut(tokens_ref, cotangent_ref, inner_ref, outer_ref)

        @pl.when(jnp.logical_not(is_first))
        def _():
            cut(tokens_ref, cotangent_ref, outer_ref, inner_ref)

    edge = ((seqs, far + near, width), tokens.dtype)
    inner, outer = call(kernel, [edge, edge], tokens, cotangent)
    return inner, lax.ppermute(outer, "ctx", pairs)


def in_order(inner, outer):
    def kernel(inner_ref, outer_ref, before_ref, after_ref):
        is_first = lax.axis_index("ctx") % 2 == 0

        @pl.when(is_first)
        def _():
            before_ref[...] = outer_ref[...]
            after_ref[...] = inner_ref[...]

        @pl.when(jnp.logical_not(is_first))
        def _():
            before_ref[...] = inner_ref[...]
            after_ref[...] = outer_ref[...]

    return call(kernel, [(inner.shape, inner.dtype)] * 2, inner, outer)


def line_slots(squares):
    def slots(z):
        slot, first, count = 0, 0, 2
        while first < squares:
            for corner in range(4):
                last = corner == 3 and first + count == squares
                for k in range(count):
                    source = square_of(z, first + k, squares)
                    yield int(last), k if last else slot, source, corner // 2, corner % 2
                    slot += 1
            first, count = first + count, first + count

    return slots


def assemble_conv(pieces, taps):
    squares = lax.axis_size("ctx") // 8
    width = pieces[0].shape[-1]
    rows = pieces[0].shape[-2] // taps

    def kernel(*refs):
        out = refs[-1]
        core, x, y, z = place()
        for dc in range(2):
            for last, slot, source, dy, dx in line_slots(squares)(z):
                for t in range(taps):
                    part = refs[2 * last + dc][slot, t * rows : (t + 1) * rows]
                    out[t, source, y ^ dy, x ^ dx, core ^ dc] = part

    out = call(kernel, [((taps, squares, 2, 2, 2, rows, width), pieces[0].dtype)], *pieces)[0]
    return out.reshape(taps, squares * 8 * rows, width)


def assemble_down(pieces, rows):
    squares = lax.axis_size("ctx") // 8
    width = pieces[0].shape[-1]

    def kernel(*refs):
        out, wide = refs[-2:]
        core, x, y, z = place()
        is_first = core == 0
        for last, slot, source, dy, dx in line_slots(squares)(z):
            mine = refs[2 * last][slot, :rows].astype(jnp.float32)
            theirs = refs[2 * last + 1][slot, :rows].astype(jnp.float32)
            wide[:rows] = jnp.where(is_first, mine, theirs)
            wide[rows:] = jnp.where(is_first, theirs, mine)
            out[source, y ^ dy, x ^ dx] = wide[...].astype(jnp.bfloat16)

    out = call(
        kernel,
        [((squares, 2, 2, 2 * rows, width), pieces[0].dtype)],
        *pieces,
        scratch=[pltpu.VMEM((2 * rows, width), jnp.float32)],
    )[0]
    return out.reshape(squares * 8 * rows, width)


def assemble_up(pieces, rows, width):
    squares = lax.axis_size("ctx") // 8

    def kernel(*refs):
        out = refs[-1]
        core, x, y, z = place()
        for piece, index, source, dy, dx, dc in up_slots(squares)(z):
            out[source, y ^ dy, x ^ dx, core ^ dc] = refs[piece][index]

    out = call(kernel, [((squares, 2, 2, 2, rows, width), pieces[0].dtype)], *pieces)[0]
    return out.reshape(squares * 8 * rows, width)


def line_masks(squares):
    return [8 << i for i in reversed(range(squares.bit_length() - 1))]


def square_of(z, slot, squares):
    for i, mask in enumerate(line_masks(squares)):
        if slot >> i & 1:
            z = z ^ (mask // 8)
    return z


def up_slots(squares):
    def slots(z):
        for core in range(2):
            for k in range(squares):
                for corner in range(4):
                    source = square_of(z, k, squares)
                    yield core, (4 * k + corner,), source, corner // 2, corner % 2, core

    return slots


def all_after(values, others):
    count = len(values)
    return lax.optimization_barrier((*values, *others))[:count]


def load(*arrays):
    count = len(arrays)

    def kernel(*refs):
        ins, outs, sem = refs[:count], refs[count:-1], refs[-1]
        copies = [pltpu.make_async_copy(i, o, sem.at[at]) for at, (i, o) in enumerate(zip(ins, outs))]
        for copy in copies:
            copy.start()
        for copy in copies:
            copy.wait()

    return pl.pallas_call(
        kernel,
        out_shape=[jax.ShapeDtypeStruct(a.shape, a.dtype) for a in arrays],
        in_specs=[pl.BlockSpec(memory_space=pltpu.HBM)] * count,
        out_specs=[VMEM] * count,
        scratch_shapes=[pltpu.SemaphoreType.DMA((count,))],
        compiler_params=PARAMS,
        cost_estimate=pl.CostEstimate(flops=1, bytes_accessed=1, transcendentals=0),
    )(*arrays)


def pack(conv_parts, down_parts, cost):
    taps, rows, width = conv_parts[0].shape
    down_rows = down_parts[0].shape[0]
    held = -(-(taps * rows + down_rows) // 16) * 16
    count = len(conv_parts)

    def kernel(*refs):
        out = refs[-1]
        for i in range(count):
            for t in range(taps):
                out[i, t * rows : (t + 1) * rows] = refs[i][t]
            out[i, taps * rows : taps * rows + down_rows] = refs[count + i][...]

    arrays = (*conv_parts, *down_parts)
    return call(kernel, [((count, held, width), conv_parts[0].dtype)], *arrays, cost=cost)[0]


def gather(conv, up, down, tokens, cotangent, prepared):
    first, *rest = line_masks(lax.axis_size("ctx") // 8)
    rows = conv.shape[0] * conv.shape[1]
    new, down_new = swap(conv, first), swap(down, first)
    up_new = [swap(up, mask) for mask in (2, 4, 6)]
    inner, outer = neighbours(*all_after((tokens, cotangent), (up_new[0],)))
    conv, up, down = load(conv, up, down)
    new, down_new, *up_new = all_after((new, down_new, *up_new), ())
    part = held = pack([conv, new], [down, down_new], cost=FIRST)
    up_held = stack([up] + up_new, cost=SECOND)
    pieces, late = [], None
    for mask, next_mask in zip([first] + rest, rest + [None]):
        count = part.shape[0]
        if late is None:
            to_x, to_y = part, part
        else:
            old, old_x, old_y = late
            to_x = join_parts((part, 0, count), (old_y, old // 2, old))
            to_y = join_parts((part, 0, count), (old_x, 0, old // 2))
        by_x, by_y, received = swap(to_x, 2), swap(to_y, 4), swap(up_held, mask)
        other = swap(inner, 1) if next_mask is None else swap(held, next_mask)
        up_held = join(up_held, received)
        if next_mask is None:
            outer = stack([outer], cost=THIRD)
        phase = (part, held, up_held, by_x, by_y, other)
        if next_mask is None:
            part, held, up_held, by_x, by_y, other, outer = all_after((*phase, outer), ())
        else:
            part, held, up_held, by_x, by_y, other = all_after(phase, ())
        if late is not None:
            pieces += [(by_y, count, count + old // 2), (by_x, count, count + old - old // 2)]
        pieces += [(part, 0, count), (by_x, 0, count), (by_y, 0, count)]
        late = (count, by_x, by_y)
        if next_mask is not None:
            held, part = join(held, other), other
    half = count // 2
    far_first = swap(join_parts((by_x, 0, half)), 4)
    far_second = swap(join_parts((by_y, half, count)), 2)
    extra = prepared(tokens, cotangent, *in_order(other, outer[0]))
    far_first = after(far_first, extra[4])
    most = join_rows(pieces, rows)
    last = join_rows([(far_first, 0, half), (far_second, 0, count - half)], rows, cost=LAST)
    pieces = [(most[0], last[0]), (up_held,), (most[1], last[1])]
    return [[both for p in piece for both in (p, swap(p, 1))] for piece in pieces], extra


def core_rows(rows):
    start = (rows // 2 - 2) // 8 * 8
    return start, rows - start


def relative_blocks(total):
    squares = lax.axis_size("ctx") // 8
    rows, width = total.shape[0] // (4 * squares), total.shape[1]
    start, held = core_rows(rows)
    blocks = total.reshape(squares, 2, 2, rows, width)

    def kernel(blocks_ref, keep_ref, send_ref):
        core, x, y, z = place()
        keep = pl.ds(pl.multiple_of(core * start, 8), held)
        send = pl.ds(pl.multiple_of((1 - core) * start, 8), held)
        for k in range(squares):
            for dy in range(2):
                for dx in range(2):
                    keep_ref[k, dy, dx] = blocks_ref[z ^ k, y ^ dy, x ^ dx, keep, :]
                    send_ref[k, dy, dx] = blocks_ref[z ^ k, y ^ dy, x ^ dx, send, :].astype(jnp.bfloat16)

    shape = (squares, 2, 2, held, width)
    return call(kernel, [(shape, jnp.float32), (shape, jnp.bfloat16)], blocks)


def chip_sums(keep, received):
    squares, _, _, held, width = keep.shape

    def kernel(keep_ref, received_ref, own_ref, x_ref, y_ref, far_ref):
        for k in range(squares):
            for corner, ref in enumerate((own_ref, x_ref, y_ref, far_ref)):
                at = (k, corner // 2, corner % 2)
                ref[k] = (keep_ref[at] + received_ref[at].astype(jnp.float32)).astype(ref.dtype)

    shape = (squares, held, width)
    return call(
        kernel, [(shape, jnp.float32)] + [(shape, jnp.bfloat16)] * 3, keep, received
    )


def line_messages(own, received, gain, each):
    squares, held, width = own.shape

    def kernel(own_ref, x_ref, y_ref, far_ref, gain_ref, sum_ref, *message_refs):
        gain = gain_ref[...]
        high = gain.astype(jnp.bfloat16).astype(jnp.float32)
        row = lax.broadcasted_iota(jnp.int32, (held, width), 0)
        row = row - jnp.where(lax.axis_index("ctx") % 2 == 0, each, 0)
        for k in range(squares):
            total = own_ref[k]
            for ref in (x_ref, y_ref, far_ref):
                total = total + ref[k].astype(jnp.float32)
            if k == 0:
                sum_ref[...] = total
            else:
                total = jnp.where(row == 0, high, jnp.where(row == 1, gain - high, total))
                message_refs[k - 1][...] = total.astype(jnp.bfloat16)

    return call(
        kernel,
        [((held, width), jnp.float32)] + [((held, width), jnp.bfloat16)] * (squares - 1),
        own,
        *received,
        gain,
    )


def finish(own, gain, received, each, factor):
    held, width = own.shape

    def kernel(own_ref, gain_ref, *refs):
        received_refs, (down_ref, out_ref) = refs[:-2], refs[-2:]
        is_first = lax.axis_index("ctx") % 2 == 0
        total, gain = own_ref[...], gain_ref[...]
        for ref in received_refs:
            terms = ref[...].astype(jnp.float32)
            total = total + terms
            high = jnp.where(is_first, terms[each : each + 1], terms[:1])
            gain = gain + (high + jnp.where(is_first, terms[each + 1 : each + 2], terms[1:2]))
        down_ref[...] = jnp.where(is_first, total[:each], total[held - each :]) * factor
        out_ref[...] = (gain * factor).reshape(width)

    return call(
        kernel,
        [((each, width), jnp.float32), ((width,), jnp.float32)],
        own,
        gain,
        *received,
    )


def body(tokens, cotangent, norm_gain, conv_weight, up_weight, down_weight, contig_first_bins):
    seqs, bins, width = tokens.shape
    ctx_count = lax.axis_size("ctx")
    data_count = lax.axis_size("dp")
    squares = ctx_count // 8
    gain = norm_gain.reshape(1, width)


    def prepared(tokens, cotangent, before, after_):
        normed = prepare(before, tokens, after_, gain, contig_first_bins)
        return (tokens, cotangent, before, after_, *normed)

    (conv_pieces, up_pieces, down_pieces), extra = gather(
        conv_weight, up_weight, down_weight, tokens, cotangent, prepared
    )
    tokens, cotangent, before, after_, taps, scaled, inverse = extra
    conv = assemble_conv(conv_pieces, conv_weight.shape[0])
    mixed = convolve(taps, tokens, conv)
    up = assemble_up(up_pieces, *up_weight.shape)
    mixed = after(mixed, *down_pieces)
    pre, share, hidden, total = expand(mixed, up, cotangent)
    slope = slopes(taps, before, after_, conv, up, pre, share)
    keep, send = relative_blocks(total)
    down = assemble_down(down_pieces, down_weight.shape[0])
    own_line, *others = chip_sums(keep, after(swap(send, 1), slope, down))
    received = [swap(v, mask) for v, mask in zip(others, (2, 4, 6))]
    mixed_grad, normed_grad, gain_term = backward(
        before, cotangent, after_, slope, down, up, conv, scaled, contig_first_bins
    )
    output, input_grad = finish_rows(
        mixed, hidden, down, mixed_grad, normed_grad, scaled, inverse, gain
    )
    for mask in (1, 2, 4):
        if mask == 4:
            gain_term = after(gain_term, output)
        gain_term = gain_term + swap(gain_term, mask)
    factor = float(ctx_count * data_count * bins * seqs) ** (-0.5)
    each = total.shape[0] // ctx_count
    own_sum, *messages = line_messages(own_line, received, gain_term, each)
    arrived = [swap(message, 8 * (k + 1)) for k, message in enumerate(messages)]
    down_part, gain_all = finish(own_sum, gain_term, arrived, each, factor)
    gain_part = gain_all
    if data_count > 1:
        width_part = width // data_count
        down_part = lax.psum_scatter(down_part, "dp", scatter_dimension=1, tiled=True)
        gain_part = lax.psum(gain_part, "dp")
        at = lax.axis_index("dp") * width_part
        gain_part = lax.dynamic_slice_in_dim(gain_part, at, width_part)
    return output, input_grad, down_part, gain_part


def solution(mesh):
    placed = (
        P("dp", "ctx", None),
        P("dp", "ctx", None),
        P(),
        P(None, "ctx", None),
        P("ctx", None),
        P("ctx", None),
        P(),
    )
    return jax.shard_map(
        body,
        mesh=mesh,
        in_specs=placed,
        out_specs=(P("dp", "ctx", None), P("dp", "ctx", None), P("ctx", "dp"), P("dp")),
        check_vma=False,
    )
```

```python
import jax
import jax.numpy as jnp
from jax import lax
from jax.experimental import pallas as pl
from jax.experimental.pallas import tpu as pltpu
from jax.sharding import PartitionSpec as P

DILATION_BINS = 64


root_half = 0.7071067811865476
inv_root_two_pi = 0.3989422804014327


def swap(value, mask):
    devices = lax.axis_size("ctx")
    return lax.ppermute(value, "ctx", [(i, i ^ mask) for i in range(devices)])


def place():
    me = lax.axis_index("ctx")
    return me % 2, (me // 2) % 2, (me // 4) % 2, me // 8


def after(value, *others):
    return lax.optimization_barrier((value,) + others)[0]


VMEM = pl.BlockSpec(memory_space=pltpu.VMEM)
FIRST, SECOND, THIRD, LAST = 5000000000, 2000000000, 4500000000, 40000000000
PARAMS = pltpu.CompilerParams(vmem_limit_bytes=20 * 1024 * 1024)

SMEM = pl.BlockSpec(memory_space=pltpu.SMEM)


def call(kernel, outs, *args, smem=(), scratch=(), cost=1):
    shapes = [jax.ShapeDtypeStruct(shape, dtype) for shape, dtype in outs]
    return pl.pallas_call(
        kernel,
        out_shape=shapes,
        in_specs=[SMEM if i in smem else VMEM for i in range(len(args))],
        out_specs=[VMEM] * len(shapes),
        scratch_shapes=list(scratch),
        compiler_params=PARAMS,
        cost_estimate=pl.CostEstimate(flops=cost, bytes_accessed=1, transcendentals=0),
    )(*args)


def segment_of(position, starts_ref):
    segment = jnp.zeros_like(position)
    for i in range(starts_ref.shape[0]):
        segment = segment + jnp.where(position >= starts_ref[i], 1, 0)
    return segment


def masks_at(first, rows, starts_ref, overall):
    position = first + lax.broadcasted_iota(jnp.int32, (rows, 1), 0)
    segment = segment_of(position, starts_ref)
    left = (position >= DILATION_BINS) & (segment_of(position - DILATION_BINS, starts_ref) == segment)
    right = (position + DILATION_BINS < overall) & (
        segment_of(position + DILATION_BINS, starts_ref) == segment
    )
    return left, right


def column_blocks(width):
    return [slice(0, width)]


def prepare(before, tokens, after_, gain, starts):
    seqs, bins, width = tokens.shape
    reach = DILATION_BINS
    overall = bins * lax.axis_size("ctx")

    def kernel(before_ref, tokens_ref, after_ref, gain_ref, starts_ref, taps_ref, scaled_ref, inverse_ref):
        first = lax.axis_index("ctx") * bins - reach
        left, right = masks_at(first, bins + 2 * reach, starts_ref, overall)
        for s in range(seqs):
            parts = []
            for ref in (before_ref, tokens_ref, after_ref):
                value = (tokens_ref[s] if ref is tokens_ref else ref[s, : 2 * reach]).astype(jnp.float32)
                inverse = lax.rsqrt(jnp.mean(value * value, axis=1, keepdims=True) + 1e-05)
                scaled = value * inverse
                if ref is tokens_ref:
                    scaled_ref[s] = scaled
                    inverse_ref[s] = inverse
                parts.append(scaled * gain_ref[...])
            normed = jnp.concatenate(parts, axis=0)
            rows = bins + 2 * reach
            taps_ref[s, :, :width] = jnp.where(left, normed[:rows], 0.0).astype(jnp.bfloat16)
            taps_ref[s, :, width : 2 * width] = normed[reach : reach + rows].astype(jnp.bfloat16)
            taps_ref[s, :, 2 * width :] = jnp.where(right, normed[2 * reach :], 0.0).astype(
                jnp.bfloat16
            )

    return call(
        kernel,
        [
            ((seqs, bins + 2 * reach, 3 * width), jnp.bfloat16),
            ((seqs, bins, width), jnp.float32),
            ((seqs, bins, 1), jnp.float32),
        ],
        before,
        tokens,
        after_,
        gain,
        starts,
        smem=(4,),
    )


def convolve(taps, tokens, conv):
    seqs, bins, width = tokens.shape
    reach = DILATION_BINS

    def kernel(taps_ref, tokens_ref, conv_ref, mixed_ref):
        for s in range(seqs):
            for at in column_blocks(width):
                mixed_ref[s, :, at] = tokens_ref[s, :, at].astype(jnp.float32) + jnp.dot(
                    taps_ref[s, reach : reach + bins],
                    conv_ref[:, at],
                    preferred_element_type=jnp.float32,
                )

    return call(
        kernel, [((seqs, bins, width), jnp.float32)], taps, tokens, conv.reshape(-1, width)
    )[0]


def expand(mixed, up, cotangent):
    seqs, bins, width = cotangent.shape
    hidden_width = up.shape[1]

    def kernel(mixed_ref, up_ref, cotangent_ref, pre_ref, share_ref, hidden_ref, total_ref):
        for s in range(seqs):
            low = mixed_ref[s].astype(jnp.bfloat16)
            for at in column_blocks(hidden_width):
                pre = jnp.dot(low, up_ref[:, at], preferred_element_type=jnp.float32)
                share = 0.5 * (1.0 + lax.erf(pre * root_half))
                hidden = (pre * share).astype(jnp.bfloat16)
                pre_ref[s, :, at] = pre
                share_ref[s, :, at] = share
                hidden_ref[s, :, at] = hidden
                term = lax.dot_general(
                    hidden,
                    cotangent_ref[s],
                    (((0,), (0,)), ((), ())),
                    preferred_element_type=jnp.float32,
                )
                if s == 0:
                    total_ref[at, :] = term
                else:
                    total_ref[at, :] += term

    return call(
        kernel,
        [
            ((seqs, bins, hidden_width), jnp.float32),
            ((seqs, bins, hidden_width), jnp.float32),
            ((seqs, bins, hidden_width), jnp.bfloat16),
            ((hidden_width, width), jnp.float32),
        ],
        mixed,
        up,
        cotangent,
    )


def slopes(taps, before, after_, conv, up, pre, share):
    seqs, bins, hidden_width = pre.shape
    width = before.shape[2]
    reach = DILATION_BINS
    rows = bins + 2 * reach

    def bell(value):
        return value * jnp.exp(-0.5 * value * value) * inv_root_two_pi

    def kernel(taps_ref, before_ref, after_ref, conv_ref, up_ref, pre_ref, share_ref, slope_ref, mixed):
        for s in range(seqs):
            edges = jnp.concatenate([taps_ref[s, :reach], taps_ref[s, reach + bins :]], axis=0)
            tokens = jnp.concatenate([before_ref[s, reach : 2 * reach], after_ref[s, :reach]], axis=0)
            for at in column_blocks(width):
                mixed[:, at] = (
                    tokens[:, at].astype(jnp.float32)
                    + jnp.dot(edges, conv_ref[:, at], preferred_element_type=jnp.float32)
                ).astype(jnp.bfloat16)
            for at in column_blocks(hidden_width):
                edge = jnp.dot(mixed[...], up_ref[:, at], preferred_element_type=jnp.float32)
                slope = 0.5 * (1.0 + lax.erf(edge * root_half)) + bell(edge)
                slope_ref[s, :reach, at] = slope[:reach]
                slope_ref[s, reach : reach + bins, at] = share_ref[s, :, at] + bell(pre_ref[s, :, at])
                slope_ref[s, reach + bins :, at] = slope[reach:]

    return call(
        kernel,
        [((seqs, rows, hidden_width), jnp.float32)],
        taps,
        before,
        after_,
        conv.reshape(-1, width),
        up,
        pre,
        share,
        scratch=[pltpu.VMEM((2 * reach, width), jnp.bfloat16)],
    )[0]


def backward(before, cotangent, after_, slope, down, up, conv, scaled, starts):
    seqs, bins, width = cotangent.shape
    hidden_width = up.shape[1]
    reach = DILATION_BINS
    rows = bins + 2 * reach
    overall = bins * lax.axis_size("ctx")
    by_rows = (((1,), (1,)), ((), ()))

    def kernel(
        before_ref,
        cotangent_ref,
        after_ref,
        slope_ref,
        down_ref,
        up_ref,
        conv_ref,
        scaled_ref,
        starts_ref,
        mixed_grad_ref,
        normed_grad_ref,
        gain_term_ref,
        pre_grad,
        mixed_grad,
    ):
        first = lax.axis_index("ctx") * bins
        left, right = masks_at(first, bins, starts_ref, overall)
        for s in range(seqs):
            cot = jnp.concatenate(
                [before_ref[s, 2 * reach :], cotangent_ref[s], after_ref[s, 2 * reach :]], axis=0
            )
            for at in column_blocks(hidden_width):
                hidden_grad = lax.dot_general(
                    cot, down_ref[at, :], by_rows, preferred_element_type=jnp.float32
                )
                pre_grad[:, at] = (hidden_grad * slope_ref[s, :, at]).astype(jnp.bfloat16)
            for at in column_blocks(width):
                mixed_grad[:, at] = cot[:, at].astype(jnp.float32) + lax.dot_general(
                    pre_grad[...], up_ref[at, :], by_rows, preferred_element_type=jnp.float32
                )
            following = jnp.where(right, mixed_grad[2 * reach :, :], 0.0).astype(jnp.bfloat16)
            center = mixed_grad[reach : reach + bins, :].astype(jnp.bfloat16)
            preceding = jnp.where(left, mixed_grad[:bins, :], 0.0).astype(jnp.bfloat16)
            mixed_grad_ref[s] = mixed_grad[reach : reach + bins, :]
            for at in column_blocks(width):
                normed_grad = (
                    lax.dot_general(following, conv_ref[0, at, :], by_rows, preferred_element_type=jnp.float32)
                    + lax.dot_general(center, conv_ref[1, at, :], by_rows, preferred_element_type=jnp.float32)
                    + lax.dot_general(preceding, conv_ref[2, at, :], by_rows, preferred_element_type=jnp.float32)
                )
                normed_grad_ref[s, :, at] = normed_grad
                term = jnp.sum(normed_grad * scaled_ref[s, :, at], axis=0, keepdims=True)
                if s == 0:
                    gain_term_ref[:, at] = term
                else:
                    gain_term_ref[:, at] += term

    return call(
        kernel,
        [
            ((seqs, bins, width), jnp.float32),
            ((seqs, bins, width), jnp.float32),
            ((1, width), jnp.float32),
        ],
        before,
        cotangent,
        after_,
        slope,
        down,
        up,
        conv,
        scaled,
        starts,
        smem=(8,),
        scratch=[
            pltpu.VMEM((rows, hidden_width), jnp.bfloat16),
            pltpu.VMEM((rows, width), jnp.float32),
        ],
    )


def finish_rows(mixed, hidden, down, mixed_grad, normed_grad, scaled, inverse, gain):
    seqs, bins, _ = hidden.shape
    width = down.shape[1]

    def kernel(
        mixed_ref,
        hidden_ref,
        down_ref,
        mixed_grad_ref,
        normed_grad_ref,
        scaled_ref,
        inverse_ref,
        gain_ref,
        out_ref,
        grad_ref,
    ):
        for s in range(seqs):
            scaled = scaled_ref[s]
            scaled_grad = normed_grad_ref[s] * gain_ref[...]
            inner = jnp.mean(scaled_grad * scaled, axis=1, keepdims=True)
            grad_ref[s] = (
                mixed_grad_ref[s] + inverse_ref[s] * (scaled_grad - scaled * inner)
            ).astype(jnp.bfloat16)
            for at in column_blocks(width):
                out_ref[s, :, at] = (
                    mixed_ref[s, :, at]
                    + jnp.dot(hidden_ref[s], down_ref[:, at], preferred_element_type=jnp.float32)
                ).astype(jnp.bfloat16)

    return call(
        kernel,
        [((seqs, bins, width), jnp.bfloat16)] * 2,
        mixed,
        hidden,
        down,
        mixed_grad,
        normed_grad,
        scaled,
        inverse,
        gain,
    )


def stack(pieces, cost=1):
    def kernel(*refs):
        for i in range(len(pieces)):
            refs[-1][i] = refs[i][...]

    shape = (len(pieces),) + pieces[0].shape
    return call(kernel, [(shape, pieces[0].dtype)], *pieces, cost=cost)[0]


def join(*pieces, cost=1):
    ends = [sum(piece.shape[0] for piece in pieces[: i + 1]) for i in range(len(pieces))]

    def kernel(*refs):
        for ref, end in zip(refs[:-1], ends):
            refs[-1][end - ref.shape[0] : end] = ref[...]

    shape = (ends[-1],) + pieces[0].shape[1:]
    return call(kernel, [(shape, pieces[0].dtype)], *pieces, cost=cost)[0]


def join_rows(pieces, rows, cost=1):
    ends = [sum(stop - start for _, start, stop in pieces[: i + 1]) for i in range(len(pieces))]
    held, width = pieces[0][0].shape[1:]

    def kernel(*refs):
        for ref, (_, start, stop), end in zip(refs[:-2], pieces, ends):
            at = slice(end - (stop - start), end)
            refs[-2][at] = ref[start:stop, :rows]
            refs[-1][at] = ref[start:stop, rows:]

    shapes = [(ends[-1], rows, width), (ends[-1], held - rows, width)]
    arrays = [piece[0] for piece in pieces]
    return call(kernel, [(shape, arrays[0].dtype) for shape in shapes], *arrays, cost=cost)


def join_parts(*pieces):
    ends = [sum(stop - start for _, start, stop in pieces[: i + 1]) for i in range(len(pieces))]

    def kernel(*refs):
        for ref, (_, start, stop), end in zip(refs[:-1], pieces, ends):
            refs[-1][end - (stop - start) : end] = ref[start:stop]

    shape = (ends[-1],) + pieces[0][0].shape[1:]
    return call(kernel, [(shape, pieces[0][0].dtype)], *[p[0] for p in pieces])[0]


def neighbours(tokens, cotangent):
    devices = lax.axis_size("ctx")
    pairs = [(i, i + 1) for i in range(1, devices - 1, 2)]
    pairs += [(j, i) for i, j in pairs]
    far, near = 2 * DILATION_BINS, DILATION_BINS
    seqs, bins, width = tokens.shape

    def cut(tokens_ref, cotangent_ref, last_ref, leading_ref):
        last_ref[:, :far] = tokens_ref[:, bins - far :]
        last_ref[:, far:] = cotangent_ref[:, bins - near :]
        leading_ref[:, :far] = tokens_ref[:, :far]
        leading_ref[:, far:] = cotangent_ref[:, :near]

    def kernel(tokens_ref, cotangent_ref, inner_ref, outer_ref):
        is_first = lax.axis_index("ctx") % 2 == 0

        @pl.when(is_first)
        def _():
            cut(tokens_ref, cotangent_ref, inner_ref, outer_ref)

        @pl.when(jnp.logical_not(is_first))
        def _():
            cut(tokens_ref, cotangent_ref, outer_ref, inner_ref)

    edge = ((seqs, far + near, width), tokens.dtype)
    inner, outer = call(kernel, [edge, edge], tokens, cotangent)
    return inner, lax.ppermute(outer, "ctx", pairs)


def in_order(inner, outer):
    def kernel(inner_ref, outer_ref, before_ref, after_ref):
        is_first = lax.axis_index("ctx") % 2 == 0

        @pl.when(is_first)
        def _():
            before_ref[...] = outer_ref[...]
            after_ref[...] = inner_ref[...]

        @pl.when(jnp.logical_not(is_first))
        def _():
            before_ref[...] = inner_ref[...]
            after_ref[...] = outer_ref[...]

    return call(kernel, [(inner.shape, inner.dtype)] * 2, inner, outer)


def line_slots(squares):
    def slots(z):
        slot, first, count = 0, 0, 2
        while first < squares:
            for corner in range(4):
                last = corner == 3 and first + count == squares
                for k in range(count):
                    source = square_of(z, first + k, squares)
                    yield int(last), k if last else slot, source, corner // 2, corner % 2
                    slot += 1
            first, count = first + count, first + count

    return slots


def assemble_conv(pieces, taps):
    squares = lax.axis_size("ctx") // 8
    width = pieces[0].shape[-1]
    rows = pieces[0].shape[-2] // taps

    def kernel(*refs):
        out = refs[-1]
        core, x, y, z = place()
        for dc in range(2):
            for last, slot, source, dy, dx in line_slots(squares)(z):
                for t in range(taps):
                    part = refs[2 * last + dc][slot, t * rows : (t + 1) * rows]
                    out[t, source, y ^ dy, x ^ dx, core ^ dc] = part

    out = call(kernel, [((taps, squares, 2, 2, 2, rows, width), pieces[0].dtype)], *pieces)[0]
    return out.reshape(taps, squares * 8 * rows, width)


def assemble_down(pieces, rows):
    squares = lax.axis_size("ctx") // 8
    width = pieces[0].shape[-1]

    def kernel(*refs):
        out, wide = refs[-2:]
        core, x, y, z = place()
        is_first = core == 0
        for last, slot, source, dy, dx in line_slots(squares)(z):
            mine = refs[2 * last][slot, :rows].astype(jnp.float32)
            theirs = refs[2 * last + 1][slot, :rows].astype(jnp.float32)
            wide[:rows] = jnp.where(is_first, mine, theirs)
            wide[rows:] = jnp.where(is_first, theirs, mine)
            out[source, y ^ dy, x ^ dx] = wide[...].astype(jnp.bfloat16)

    out = call(
        kernel,
        [((squares, 2, 2, 2 * rows, width), pieces[0].dtype)],
        *pieces,
        scratch=[pltpu.VMEM((2 * rows, width), jnp.float32)],
    )[0]
    return out.reshape(squares * 8 * rows, width)


def assemble_up(pieces, rows, width):
    squares = lax.axis_size("ctx") // 8

    def kernel(*refs):
        out = refs[-1]
        core, x, y, z = place()
        for piece, index, source, dy, dx, dc in up_slots(squares)(z):
            out[source, y ^ dy, x ^ dx, core ^ dc] = refs[piece][index]

    out = call(kernel, [((squares, 2, 2, 2, rows, width), pieces[0].dtype)], *pieces)[0]
    return out.reshape(squares * 8 * rows, width)


def line_masks(squares):
    return [8 << i for i in reversed(range(squares.bit_length() - 1))]


def square_of(z, slot, squares):
    for i, mask in enumerate(line_masks(squares)):
        if slot >> i & 1:
            z = z ^ (mask // 8)
    return z


def up_slots(squares):
    def slots(z):
        for core in range(2):
            for k in range(squares):
                for corner in range(4):
                    source = square_of(z, k, squares)
                    yield core, (4 * k + corner,), source, corner // 2, corner % 2, core

    return slots


def all_after(values, others):
    count = len(values)
    return lax.optimization_barrier((*values, *others))[:count]


def load(*arrays):
    count = len(arrays)

    def kernel(*refs):
        ins, outs, sem = refs[:count], refs[count:-1], refs[-1]
        copies = [pltpu.make_async_copy(i, o, sem.at[at]) for at, (i, o) in enumerate(zip(ins, outs))]
        for copy in copies:
            copy.start()
        for copy in copies:
            copy.wait()

    return pl.pallas_call(
        kernel,
        out_shape=[jax.ShapeDtypeStruct(a.shape, a.dtype) for a in arrays],
        in_specs=[pl.BlockSpec(memory_space=pltpu.HBM)] * count,
        out_specs=[VMEM] * count,
        scratch_shapes=[pltpu.SemaphoreType.DMA((count,))],
        compiler_params=PARAMS,
        cost_estimate=pl.CostEstimate(flops=1, bytes_accessed=1, transcendentals=0),
    )(*arrays)


def pack(conv_parts, down_parts, cost):
    taps, rows, width = conv_parts[0].shape
    down_rows = down_parts[0].shape[0]
    held = -(-(taps * rows + down_rows) // 16) * 16
    count = len(conv_parts)

    def kernel(*refs):
        out = refs[-1]
        for i in range(count):
            for t in range(taps):
                out[i, t * rows : (t + 1) * rows] = refs[i][t]
            out[i, taps * rows : taps * rows + down_rows] = refs[count + i][...]

    arrays = (*conv_parts, *down_parts)
    return call(kernel, [((count, held, width), conv_parts[0].dtype)], *arrays, cost=cost)[0]


def gather(conv, up, down, tokens, cotangent, prepared):
    first, *rest = line_masks(lax.axis_size("ctx") // 8)
    rows = conv.shape[0] * conv.shape[1]
    new, down_new = swap(conv, first), swap(down, first)
    up_new = [swap(up, mask) for mask in (2, 4, 6)]
    inner, outer = neighbours(*all_after((tokens, cotangent), (up_new[0],)))
    conv, up, down = load(conv, up, down)
    new, down_new, *up_new = all_after((new, down_new, *up_new), ())
    part = held = pack([conv, new], [down, down_new], cost=FIRST)
    up_held = stack([up] + up_new, cost=SECOND)
    pieces, late = [], None
    for mask, next_mask in zip([first] + rest, rest + [None]):
        count = part.shape[0]
        if late is None:
            to_x, to_y = part, part
        else:
            old, old_x, old_y = late
            to_x = join_parts((part, 0, count), (old_y, old // 2, old))
            to_y = join_parts((part, 0, count), (old_x, 0, old // 2))
        by_x, by_y, received = swap(to_x, 2), swap(to_y, 4), swap(up_held, mask)
        other = swap(inner, 1) if next_mask is None else swap(held, next_mask)
        up_held = join(up_held, received)
        if next_mask is None:
            outer = stack([outer], cost=THIRD)
        phase = (part, held, up_held, by_x, by_y, other)
        if next_mask is None:
            part, held, up_held, by_x, by_y, other, outer = all_after((*phase, outer), ())
        else:
            part, held, up_held, by_x, by_y, other = all_after(phase, ())
        if late is not None:
            pieces += [(by_y, count, count + old // 2), (by_x, count, count + old - old // 2)]
        pieces += [(part, 0, count), (by_x, 0, count), (by_y, 0, count)]
        late = (count, by_x, by_y)
        if next_mask is not None:
            held, part = join(held, other), other
    half = count // 2
    far_first = swap(join_parts((by_x, 0, half)), 4)
    far_second = swap(join_parts((by_y, half, count)), 2)
    extra = prepared(tokens, cotangent, *in_order(other, outer[0]))
    far_first = after(far_first, extra[4])
    most = join_rows(pieces, rows)
    last = join_rows([(far_first, 0, half), (far_second, 0, count - half)], rows, cost=LAST)
    pieces = [(most[0], last[0]), (up_held,), (most[1], last[1])]
    return [[both for p in piece for both in (p, swap(p, 1))] for piece in pieces], extra


def core_rows(rows):
    start = (rows // 2 - 2) // 8 * 8
    return start, rows - start


def relative_blocks(total):
    squares = lax.axis_size("ctx") // 8
    rows, width = total.shape[0] // (4 * squares), total.shape[1]
    start, held = core_rows(rows)
    blocks = total.reshape(squares, 2, 2, rows, width)

    def kernel(blocks_ref, keep_ref, send_ref):
        core, x, y, z = place()
        keep = pl.ds(pl.multiple_of(core * start, 8), held)
        send = pl.ds(pl.multiple_of((1 - core) * start, 8), held)
        for k in range(squares):
            for dy in range(2):
                for dx in range(2):
                    keep_ref[k, dy, dx] = blocks_ref[z ^ k, y ^ dy, x ^ dx, keep, :]
                    send_ref[k, dy, dx] = blocks_ref[z ^ k, y ^ dy, x ^ dx, send, :].astype(jnp.bfloat16)

    shape = (squares, 2, 2, held, width)
    return call(kernel, [(shape, jnp.float32), (shape, jnp.bfloat16)], blocks)


def chip_sums(keep, received):
    squares, _, _, held, width = keep.shape

    def kernel(keep_ref, received_ref, own_ref, x_ref, y_ref, far_ref):
        for k in range(squares):
            for corner, ref in enumerate((own_ref, x_ref, y_ref, far_ref)):
                at = (k, corner // 2, corner % 2)
                ref[k] = (keep_ref[at] + received_ref[at].astype(jnp.float32)).astype(ref.dtype)

    shape = (squares, held, width)
    return call(
        kernel, [(shape, jnp.float32)] + [(shape, jnp.bfloat16)] * 3, keep, received
    )


def line_messages(own, received, gain, each):
    squares, held, width = own.shape

    def kernel(own_ref, x_ref, y_ref, far_ref, gain_ref, sum_ref, *message_refs):
        gain = gain_ref[...]
        high = gain.astype(jnp.bfloat16).astype(jnp.float32)
        row = lax.broadcasted_iota(jnp.int32, (held, width), 0)
        row = row - jnp.where(lax.axis_index("ctx") % 2 == 0, each, 0)
        for k in range(squares):
            total = own_ref[k]
            for ref in (x_ref, y_ref, far_ref):
                total = total + ref[k].astype(jnp.float32)
            if k == 0:
                sum_ref[...] = total
            else:
                total = jnp.where(row == 0, high, jnp.where(row == 1, gain - high, total))
                message_refs[k - 1][...] = total.astype(jnp.bfloat16)

    return call(
        kernel,
        [((held, width), jnp.float32)] + [((held, width), jnp.bfloat16)] * (squares - 1),
        own,
        *received,
        gain,
    )


def finish(own, gain, received, each, factor):
    held, width = own.shape

    def kernel(own_ref, gain_ref, *refs):
        received_refs, (down_ref, out_ref) = refs[:-2], refs[-2:]
        is_first = lax.axis_index("ctx") % 2 == 0
        total, gain = own_ref[...], gain_ref[...]
        for ref in received_refs:
            terms = ref[...].astype(jnp.float32)
            total = total + terms
            high = jnp.where(is_first, terms[each : each + 1], terms[:1])
            gain = gain + (high + jnp.where(is_first, terms[each + 1 : each + 2], terms[1:2]))
        down_ref[...] = jnp.where(is_first, total[:each], total[held - each :]) * factor
        out_ref[...] = (gain * factor).reshape(width)

    return call(
        kernel,
        [((each, width), jnp.float32), ((width,), jnp.float32)],
        own,
        gain,
        *received,
    )


def body(tokens, cotangent, norm_gain, conv_weight, up_weight, down_weight, contig_first_bins):
    seqs, bins, width = tokens.shape
    ctx_count = lax.axis_size("ctx")
    data_count = lax.axis_size("dp")
    squares = ctx_count // 8
    gain = norm_gain.reshape(1, width)


    def prepared(tokens, cotangent, before, after_):
        normed = prepare(before, tokens, after_, gain, contig_first_bins)
        return (tokens, cotangent, before, after_, *normed)

    (conv_pieces, up_pieces, down_pieces), extra = gather(
        conv_weight, up_weight, down_weight, tokens, cotangent, prepared
    )
    tokens, cotangent, before, after_, taps, scaled, inverse = extra
    conv = assemble_conv(conv_pieces, conv_weight.shape[0])
    mixed = convolve(taps, tokens, conv)
    up = assemble_up(up_pieces, *up_weight.shape)
    mixed = after(mixed, *down_pieces)
    pre, share, hidden, total = expand(mixed, up, cotangent)
    slope = slopes(taps, before, after_, conv, up, pre, share)
    keep, send = relative_blocks(total)
    down = assemble_down(down_pieces, down_weight.shape[0])
    own_line, *others = chip_sums(keep, after(swap(send, 1), slope, down))
    received = [swap(v, mask) for v, mask in zip(others, (2, 4, 6))]
    mixed_grad, normed_grad, gain_term = backward(
        before, cotangent, after_, slope, down, up, conv, scaled, contig_first_bins
    )
    output, input_grad = finish_rows(
        mixed, hidden, down, mixed_grad, normed_grad, scaled, inverse, gain
    )
    for mask in (1, 2, 4):
        if mask == 4:
            gain_term = after(gain_term, output)
        gain_term = gain_term + swap(gain_term, mask)
    factor = float(ctx_count * data_count * bins * seqs) ** (-0.5)
    each = total.shape[0] // ctx_count
    own_sum, *messages = line_messages(own_line, received, gain_term, each)
    arrived = [swap(message, 8 * (k + 1)) for k, message in enumerate(messages)]
    down_part, gain_all = finish(own_sum, gain_term, arrived, each, factor)
    gain_part = gain_all
    if data_count > 1:
        width_part = width // data_count
        down_part = lax.psum_scatter(down_part, "dp", scatter_dimension=1, tiled=True)
        gain_part = lax.psum(gain_part, "dp")
        at = lax.axis_index("dp") * width_part
        gain_part = lax.dynamic_slice_in_dim(gain_part, at, width_part)
    return output, input_grad, down_part, gain_part


def solution(mesh):
    placed = (
        P("dp", "ctx", None),
        P("dp", "ctx", None),
        P(),
        P(None, "ctx", None),
        P("ctx", None),
        P("ctx", None),
        P(),
    )
    return jax.shard_map(
        body,
        mesh=mesh,
        in_specs=placed,
        out_specs=(P("dp", "ctx", None), P("dp", "ctx", None), P("ctx", "dp"), P("dp")),
        check_vma=False,
    )
```

```python
import jax
import jax.numpy as jnp
from jax import lax
from jax.experimental import pallas as pl
from jax.experimental.pallas import tpu as pltpu
from jax.sharding import PartitionSpec as P

DILATION_BINS = 64


root_half = 0.7071067811865476
inv_root_two_pi = 0.3989422804014327


def swap(value, mask):
    devices = lax.axis_size("ctx")
    return lax.ppermute(value, "ctx", [(i, i ^ mask) for i in range(devices)])


def place():
    me = lax.axis_index("ctx")
    return me % 2, (me // 2) % 2, (me // 4) % 2, me // 8


def after(value, *others):
    return lax.optimization_barrier((value,) + others)[0]


VMEM = pl.BlockSpec(memory_space=pltpu.VMEM)
FIRST, SECOND, THIRD, LAST = 5000000000, 2000000000, 4500000000, 40000000000
PARAMS = pltpu.CompilerParams(vmem_limit_bytes=20 * 1024 * 1024)

SMEM = pl.BlockSpec(memory_space=pltpu.SMEM)


def call(kernel, outs, *args, smem=(), scratch=(), cost=1):
    shapes = [jax.ShapeDtypeStruct(shape, dtype) for shape, dtype in outs]
    return pl.pallas_call(
        kernel,
        out_shape=shapes,
        in_specs=[SMEM if i in smem else VMEM for i in range(len(args))],
        out_specs=[VMEM] * len(shapes),
        scratch_shapes=list(scratch),
        compiler_params=PARAMS,
        cost_estimate=pl.CostEstimate(flops=cost, bytes_accessed=1, transcendentals=0),
    )(*args)


def segment_of(position, starts_ref):
    segment = jnp.zeros_like(position)
    for i in range(starts_ref.shape[0]):
        segment = segment + jnp.where(position >= starts_ref[i], 1, 0)
    return segment


def masks_at(first, rows, starts_ref, overall):
    position = first + lax.broadcasted_iota(jnp.int32, (rows, 1), 0)
    segment = segment_of(position, starts_ref)
    left = (position >= DILATION_BINS) & (segment_of(position - DILATION_BINS, starts_ref) == segment)
    right = (position + DILATION_BINS < overall) & (
        segment_of(position + DILATION_BINS, starts_ref) == segment
    )
    return left, right


def column_blocks(width):
    return [slice(0, width)]


def prepare(before, tokens, after_, gain, starts):
    seqs, bins, width = tokens.shape
    reach = DILATION_BINS
    overall = bins * lax.axis_size("ctx")

    def kernel(before_ref, tokens_ref, after_ref, gain_ref, starts_ref, taps_ref, scaled_ref, inverse_ref):
        first = lax.axis_index("ctx") * bins - reach
        left, right = masks_at(first, bins + 2 * reach, starts_ref, overall)
        for s in range(seqs):
            parts = []
            for ref in (before_ref, tokens_ref, after_ref):
                value = (tokens_ref[s] if ref is tokens_ref else ref[s, : 2 * reach]).astype(jnp.float32)
                inverse = lax.rsqrt(jnp.mean(value * value, axis=1, keepdims=True) + 1e-05)
                scaled = value * inverse
                if ref is tokens_ref:
                    scaled_ref[s] = scaled
                    inverse_ref[s] = inverse
                parts.append(scaled * gain_ref[...])
            normed = jnp.concatenate(parts, axis=0)
            rows = bins + 2 * reach
            taps_ref[s, :, :width] = jnp.where(left, normed[:rows], 0.0).astype(jnp.bfloat16)
            taps_ref[s, :, width : 2 * width] = normed[reach : reach + rows].astype(jnp.bfloat16)
            taps_ref[s, :, 2 * width :] = jnp.where(right, normed[2 * reach :], 0.0).astype(
                jnp.bfloat16
            )

    return call(
        kernel,
        [
            ((seqs, bins + 2 * reach, 3 * width), jnp.bfloat16),
            ((seqs, bins, width), jnp.float32),
            ((seqs, bins, 1), jnp.float32),
        ],
        before,
        tokens,
        after_,
        gain,
        starts,
        smem=(4,),
    )


def convolve(taps, tokens, conv):
    seqs, bins, width = tokens.shape
    reach = DILATION_BINS

    def kernel(taps_ref, tokens_ref, conv_ref, mixed_ref):
        for s in range(seqs):
            for at in column_blocks(width):
                mixed_ref[s, :, at] = tokens_ref[s, :, at].astype(jnp.float32) + jnp.dot(
                    taps_ref[s, reach : reach + bins],
                    conv_ref[:, at],
                    preferred_element_type=jnp.float32,
                )

    return call(
        kernel, [((seqs, bins, width), jnp.float32)], taps, tokens, conv.reshape(-1, width)
    )[0]


def expand(mixed, up, cotangent):
    seqs, bins, width = cotangent.shape
    hidden_width = up.shape[1]

    def kernel(mixed_ref, up_ref, cotangent_ref, pre_ref, share_ref, hidden_ref, total_ref):
        for s in range(seqs):
            low = mixed_ref[s].astype(jnp.bfloat16)
            for at in column_blocks(hidden_width):
                pre = jnp.dot(low, up_ref[:, at], preferred_element_type=jnp.float32)
                share = 0.5 * (1.0 + lax.erf(pre * root_half))
                hidden = (pre * share).astype(jnp.bfloat16)
                pre_ref[s, :, at] = pre
                share_ref[s, :, at] = share
                hidden_ref[s, :, at] = hidden
                term = lax.dot_general(
                    hidden,
                    cotangent_ref[s],
                    (((0,), (0,)), ((), ())),
                    preferred_element_type=jnp.float32,
                )
                if s == 0:
                    total_ref[at, :] = term
                else:
                    total_ref[at, :] += term

    return call(
        kernel,
        [
            ((seqs, bins, hidden_width), jnp.float32),
            ((seqs, bins, hidden_width), jnp.float32),
            ((seqs, bins, hidden_width), jnp.bfloat16),
            ((hidden_width, width), jnp.float32),
        ],
        mixed,
        up,
        cotangent,
    )


def slopes(taps, before, after_, conv, up, pre, share):
    seqs, bins, hidden_width = pre.shape
    width = before.shape[2]
    reach = DILATION_BINS
    rows = bins + 2 * reach

    def bell(value):
        return value * jnp.exp(-0.5 * value * value) * inv_root_two_pi

    def kernel(taps_ref, before_ref, after_ref, conv_ref, up_ref, pre_ref, share_ref, slope_ref, mixed):
        for s in range(seqs):
            edges = jnp.concatenate([taps_ref[s, :reach], taps_ref[s, reach + bins :]], axis=0)
            tokens = jnp.concatenate([before_ref[s, reach : 2 * reach], after_ref[s, :reach]], axis=0)
            for at in column_blocks(width):
                mixed[:, at] = (
                    tokens[:, at].astype(jnp.float32)
                    + jnp.dot(edges, conv_ref[:, at], preferred_element_type=jnp.float32)
                ).astype(jnp.bfloat16)
            for at in column_blocks(hidden_width):
                edge = jnp.dot(mixed[...], up_ref[:, at], preferred_element_type=jnp.float32)
                slope = 0.5 * (1.0 + lax.erf(edge * root_half)) + bell(edge)
                slope_ref[s, :reach, at] = slope[:reach]
                slope_ref[s, reach : reach + bins, at] = share_ref[s, :, at] + bell(pre_ref[s, :, at])
                slope_ref[s, reach + bins :, at] = slope[reach:]

    return call(
        kernel,
        [((seqs, rows, hidden_width), jnp.float32)],
        taps,
        before,
        after_,
        conv.reshape(-1, width),
        up,
        pre,
        share,
        scratch=[pltpu.VMEM((2 * reach, width), jnp.bfloat16)],
    )[0]


def backward(before, cotangent, after_, slope, down, up, conv, scaled, starts):
    seqs, bins, width = cotangent.shape
    hidden_width = up.shape[1]
    reach = DILATION_BINS
    rows = bins + 2 * reach
    overall = bins * lax.axis_size("ctx")
    by_rows = (((1,), (1,)), ((), ()))

    def kernel(
        before_ref,
        cotangent_ref,
        after_ref,
        slope_ref,
        down_ref,
        up_ref,
        conv_ref,
        scaled_ref,
        starts_ref,
        mixed_grad_ref,
        normed_grad_ref,
        gain_term_ref,
        pre_grad,
        mixed_grad,
    ):
        first = lax.axis_index("ctx") * bins
        left, right = masks_at(first, bins, starts_ref, overall)
        for s in range(seqs):
            cot = jnp.concatenate(
                [before_ref[s, 2 * reach :], cotangent_ref[s], after_ref[s, 2 * reach :]], axis=0
            )
            for at in column_blocks(hidden_width):
                hidden_grad = lax.dot_general(
                    cot, down_ref[at, :], by_rows, preferred_element_type=jnp.float32
                )
                pre_grad[:, at] = (hidden_grad * slope_ref[s, :, at]).astype(jnp.bfloat16)
            for at in column_blocks(width):
                mixed_grad[:, at] = cot[:, at].astype(jnp.float32) + lax.dot_general(
                    pre_grad[...], up_ref[at, :], by_rows, preferred_element_type=jnp.float32
                )
            following = jnp.where(right, mixed_grad[2 * reach :, :], 0.0).astype(jnp.bfloat16)
            center = mixed_grad[reach : reach + bins, :].astype(jnp.bfloat16)
            preceding = jnp.where(left, mixed_grad[:bins, :], 0.0).astype(jnp.bfloat16)
            mixed_grad_ref[s] = mixed_grad[reach : reach + bins, :]
            for at in column_blocks(width):
                normed_grad = (
                    lax.dot_general(following, conv_ref[0, at, :], by_rows, preferred_element_type=jnp.float32)
                    + lax.dot_general(center, conv_ref[1, at, :], by_rows, preferred_element_type=jnp.float32)
                    + lax.dot_general(preceding, conv_ref[2, at, :], by_rows, preferred_element_type=jnp.float32)
                )
                normed_grad_ref[s, :, at] = normed_grad
                term = jnp.sum(normed_grad * scaled_ref[s, :, at], axis=0, keepdims=True)
                if s == 0:
                    gain_term_ref[:, at] = term
                else:
                    gain_term_ref[:, at] += term

    return call(
        kernel,
        [
            ((seqs, bins, width), jnp.float32),
            ((seqs, bins, width), jnp.float32),
            ((1, width), jnp.float32),
        ],
        before,
        cotangent,
        after_,
        slope,
        down,
        up,
        conv,
        scaled,
        starts,
        smem=(8,),
        scratch=[
            pltpu.VMEM((rows, hidden_width), jnp.bfloat16),
            pltpu.VMEM((rows, width), jnp.float32),
        ],
    )


def finish_rows(mixed, hidden, down, mixed_grad, normed_grad, scaled, inverse, gain):
    seqs, bins, _ = hidden.shape
    width = down.shape[1]

    def kernel(
        mixed_ref,
        hidden_ref,
        down_ref,
        mixed_grad_ref,
        normed_grad_ref,
        scaled_ref,
        inverse_ref,
        gain_ref,
        out_ref,
        grad_ref,
    ):
        for s in range(seqs):
            scaled = scaled_ref[s]
            scaled_grad = normed_grad_ref[s] * gain_ref[...]
            inner = jnp.mean(scaled_grad * scaled, axis=1, keepdims=True)
            grad_ref[s] = (
                mixed_grad_ref[s] + inverse_ref[s] * (scaled_grad - scaled * inner)
            ).astype(jnp.bfloat16)
            for at in column_blocks(width):
                out_ref[s, :, at] = (
                    mixed_ref[s, :, at]
                    + jnp.dot(hidden_ref[s], down_ref[:, at], preferred_element_type=jnp.float32)
                ).astype(jnp.bfloat16)

    return call(
        kernel,
        [((seqs, bins, width), jnp.bfloat16)] * 2,
        mixed,
        hidden,
        down,
        mixed_grad,
        normed_grad,
        scaled,
        inverse,
        gain,
    )


def stack(pieces, cost=1):
    def kernel(*refs):
        for i in range(len(pieces)):
            refs[-1][i] = refs[i][...]

    shape = (len(pieces),) + pieces[0].shape
    return call(kernel, [(shape, pieces[0].dtype)], *pieces, cost=cost)[0]


def join(*pieces, cost=1):
    ends = [sum(piece.shape[0] for piece in pieces[: i + 1]) for i in range(len(pieces))]

    def kernel(*refs):
        for ref, end in zip(refs[:-1], ends):
            refs[-1][end - ref.shape[0] : end] = ref[...]

    shape = (ends[-1],) + pieces[0].shape[1:]
    return call(kernel, [(shape, pieces[0].dtype)], *pieces, cost=cost)[0]


def join_rows(pieces, rows, cost=1):
    ends = [sum(stop - start for _, start, stop in pieces[: i + 1]) for i in range(len(pieces))]
    held, width = pieces[0][0].shape[1:]

    def kernel(*refs):
        for ref, (_, start, stop), end in zip(refs[:-2], pieces, ends):
            at = slice(end - (stop - start), end)
            refs[-2][at] = ref[start:stop, :rows]
            refs[-1][at] = ref[start:stop, rows:]

    shapes = [(ends[-1], rows, width), (ends[-1], held - rows, width)]
    arrays = [piece[0] for piece in pieces]
    return call(kernel, [(shape, arrays[0].dtype) for shape in shapes], *arrays, cost=cost)


def join_parts(*pieces):
    ends = [sum(stop - start for _, start, stop in pieces[: i + 1]) for i in range(len(pieces))]

    def kernel(*refs):
        for ref, (_, start, stop), end in zip(refs[:-1], pieces, ends):
            refs[-1][end - (stop - start) : end] = ref[start:stop]

    shape = (ends[-1],) + pieces[0][0].shape[1:]
    return call(kernel, [(shape, pieces[0][0].dtype)], *[p[0] for p in pieces])[0]


def neighbours(tokens, cotangent):
    devices = lax.axis_size("ctx")
    pairs = [(i, i + 1) for i in range(1, devices - 1, 2)]
    pairs += [(j, i) for i, j in pairs]
    far, near = 2 * DILATION_BINS, DILATION_BINS
    seqs, bins, width = tokens.shape

    def cut(tokens_ref, cotangent_ref, last_ref, leading_ref):
        last_ref[:, :far] = tokens_ref[:, bins - far :]
        last_ref[:, far:] = cotangent_ref[:, bins - near :]
        leading_ref[:, :far] = tokens_ref[:, :far]
        leading_ref[:, far:] = cotangent_ref[:, :near]

    def kernel(tokens_ref, cotangent_ref, inner_ref, outer_ref):
        is_first = lax.axis_index("ctx") % 2 == 0

        @pl.when(is_first)
        def _():
            cut(tokens_ref, cotangent_ref, inner_ref, outer_ref)

        @pl.when(jnp.logical_not(is_first))
        def _():
            cut(tokens_ref, cotangent_ref, outer_ref, inner_ref)

    edge = ((seqs, far + near, width), tokens.dtype)
    inner, outer = call(kernel, [edge, edge], tokens, cotangent)
    return inner, lax.ppermute(outer, "ctx", pairs)


def in_order(inner, outer):
    def kernel(inner_ref, outer_ref, before_ref, after_ref):
        is_first = lax.axis_index("ctx") % 2 == 0

        @pl.when(is_first)
        def _():
            before_ref[...] = outer_ref[...]
            after_ref[...] = inner_ref[...]

        @pl.when(jnp.logical_not(is_first))
        def _():
            before_ref[...] = inner_ref[...]
            after_ref[...] = outer_ref[...]

    return call(kernel, [(inner.shape, inner.dtype)] * 2, inner, outer)


def line_slots(squares):
    def slots(z):
        slot, first, count = 0, 0, 2
        while first < squares:
            for corner in range(4):
                last = corner == 3 and first + count == squares
                for k in range(count):
                    source = square_of(z, first + k, squares)
                    yield int(last), k if last else slot, source, corner // 2, corner % 2
                    slot += 1
            first, count = first + count, first + count

    return slots


def assemble_conv(pieces, taps):
    squares = lax.axis_size("ctx") // 8
    width = pieces[0].shape[-1]
    rows = pieces[0].shape[-2] // taps

    def kernel(*refs):
        out = refs[-1]
        core, x, y, z = place()
        for dc in range(2):
            for last, slot, source, dy, dx in line_slots(squares)(z):
                for t in range(taps):
                    part = refs[2 * last + dc][slot, t * rows : (t + 1) * rows]
                    out[t, source, y ^ dy, x ^ dx, core ^ dc] = part

    out = call(kernel, [((taps, squares, 2, 2, 2, rows, width), pieces[0].dtype)], *pieces)[0]
    return out.reshape(taps, squares * 8 * rows, width)


def assemble_down(pieces, rows):
    squares = lax.axis_size("ctx") // 8
    width = pieces[0].shape[-1]

    def kernel(*refs):
        out, wide = refs[-2:]
        core, x, y, z = place()
        is_first = core == 0
        for last, slot, source, dy, dx in line_slots(squares)(z):
            mine = refs[2 * last][slot, :rows].astype(jnp.float32)
            theirs = refs[2 * last + 1][slot, :rows].astype(jnp.float32)
            wide[:rows] = jnp.where(is_first, mine, theirs)
            wide[rows:] = jnp.where(is_first, theirs, mine)
            out[source, y ^ dy, x ^ dx] = wide[...].astype(jnp.bfloat16)

    out = call(
        kernel,
        [((squares, 2, 2, 2 * rows, width), pieces[0].dtype)],
        *pieces,
        scratch=[pltpu.VMEM((2 * rows, width), jnp.float32)],
    )[0]
    return out.reshape(squares * 8 * rows, width)


def assemble_up(pieces, rows, width):
    squares = lax.axis_size("ctx") // 8

    def kernel(*refs):
        out = refs[-1]
        core, x, y, z = place()
        for piece, index, source, dy, dx, dc in up_slots(squares)(z):
            out[source, y ^ dy, x ^ dx, core ^ dc] = refs[piece][index]

    out = call(kernel, [((squares, 2, 2, 2, rows, width), pieces[0].dtype)], *pieces)[0]
    return out.reshape(squares * 8 * rows, width)


def line_masks(squares):
    return [8 << i for i in reversed(range(squares.bit_length() - 1))]


def square_of(z, slot, squares):
    for i, mask in enumerate(line_masks(squares)):
        if slot >> i & 1:
            z = z ^ (mask // 8)
    return z


def up_slots(squares):
    def slots(z):
        for core in range(2):
            for k in range(squares):
                for corner in range(4):
                    source = square_of(z, k, squares)
                    yield core, (4 * k + corner,), source, corner // 2, corner % 2, core

    return slots


def all_after(values, others):
    count = len(values)
    return lax.optimization_barrier((*values, *others))[:count]


def load(*arrays):
    count = len(arrays)

    def kernel(*refs):
        ins, outs, sem = refs[:count], refs[count:-1], refs[-1]
        copies = [pltpu.make_async_copy(i, o, sem.at[at]) for at, (i, o) in enumerate(zip(ins, outs))]
        for copy in copies:
            copy.start()
        for copy in copies:
            copy.wait()

    return pl.pallas_call(
        kernel,
        out_shape=[jax.ShapeDtypeStruct(a.shape, a.dtype) for a in arrays],
        in_specs=[pl.BlockSpec(memory_space=pltpu.HBM)] * count,
        out_specs=[VMEM] * count,
        scratch_shapes=[pltpu.SemaphoreType.DMA((count,))],
        compiler_params=PARAMS,
        cost_estimate=pl.CostEstimate(flops=1, bytes_accessed=1, transcendentals=0),
    )(*arrays)


def pack(conv_parts, down_parts, cost):
    taps, rows, width = conv_parts[0].shape
    down_rows = down_parts[0].shape[0]
    held = -(-(taps * rows + down_rows) // 16) * 16
    count = len(conv_parts)

    def kernel(*refs):
        out = refs[-1]
        for i in range(count):
            for t in range(taps):
                out[i, t * rows : (t + 1) * rows] = refs[i][t]
            out[i, taps * rows : taps * rows + down_rows] = refs[count + i][...]

    arrays = (*conv_parts, *down_parts)
    return call(kernel, [((count, held, width), conv_parts[0].dtype)], *arrays, cost=cost)[0]


def gather(conv, up, down, tokens, cotangent, prepared):
    first, *rest = line_masks(lax.axis_size("ctx") // 8)
    rows = conv.shape[0] * conv.shape[1]
    new, down_new = swap(conv, first), swap(down, first)
    up_new = [swap(up, mask) for mask in (2, 4, 6)]
    inner, outer = neighbours(*all_after((tokens, cotangent), (up_new[0],)))
    conv, up, down = load(conv, up, down)
    new, down_new, *up_new = all_after((new, down_new, *up_new), ())
    part = held = pack([conv, new], [down, down_new], cost=FIRST)
    up_held = stack([up] + up_new, cost=SECOND)
    pieces, late = [], None
    for mask, next_mask in zip([first] + rest, rest + [None]):
        count = part.shape[0]
        if late is None:
            to_x, to_y = part, part
        else:
            old, old_x, old_y = late
            to_x = join_parts((part, 0, count), (old_y, old // 2, old))
            to_y = join_parts((part, 0, count), (old_x, 0, old // 2))
        by_x, by_y, received = swap(to_x, 2), swap(to_y, 4), swap(up_held, mask)
        other = swap(inner, 1) if next_mask is None else swap(held, next_mask)
        up_held = join(up_held, received, cost=1 if next_mask is None else 1_500_000_000)
        if next_mask is None:
            outer = stack([outer], cost=THIRD)
        phase = (part, held, up_held, by_x, by_y, other)
        if next_mask is None:
            part, held, up_held, by_x, by_y, other, outer = all_after((*phase, outer), ())
        else:
            part, held, up_held, by_x, by_y, other = all_after(phase, ())
        if late is not None:
            pieces += [(by_y, count, count + old // 2), (by_x, count, count + old - old // 2)]
        pieces += [(part, 0, count), (by_x, 0, count), (by_y, 0, count)]
        late = (count, by_x, by_y)
        if next_mask is not None:
            held, part = join(held, other), other
    half = count // 2
    far_first = swap(join_parts((by_x, 0, half)), 4)
    far_second = swap(join_parts((by_y, half, count)), 2)
    extra = prepared(tokens, cotangent, *in_order(other, outer[0]))
    far_first = after(far_first, extra[4])
    most = join_rows(pieces, rows)
    last = join_rows([(far_first, 0, half), (far_second, 0, count - half)], rows, cost=LAST)
    pieces = [(most[0], last[0]), (up_held,), (most[1], last[1])]
    return [[both for p in piece for both in (p, swap(p, 1))] for piece in pieces], extra


def core_rows(rows):
    start = (rows // 2 - 2) // 8 * 8
    return start, rows - start


def relative_blocks(total):
    squares = lax.axis_size("ctx") // 8
    rows, width = total.shape[0] // (4 * squares), total.shape[1]
    start, held = core_rows(rows)
    blocks = total.reshape(squares, 2, 2, rows, width)

    def kernel(blocks_ref, keep_ref, send_ref):
        core, x, y, z = place()
        keep = pl.ds(pl.multiple_of(core * start, 8), held)
        send = pl.ds(pl.multiple_of((1 - core) * start, 8), held)
        for k in range(squares):
            for dy in range(2):
                for dx in range(2):
                    keep_ref[k, dy, dx] = blocks_ref[z ^ k, y ^ dy, x ^ dx, keep, :]
                    send_ref[k, dy, dx] = blocks_ref[z ^ k, y ^ dy, x ^ dx, send, :].astype(jnp.bfloat16)

    shape = (squares, 2, 2, held, width)
    return call(kernel, [(shape, jnp.float32), (shape, jnp.bfloat16)], blocks)


def chip_sums(keep, received):
    squares, _, _, held, width = keep.shape

    def kernel(keep_ref, received_ref, own_ref, x_ref, y_ref, far_ref):
        for k in range(squares):
            for corner, ref in enumerate((own_ref, x_ref, y_ref, far_ref)):
                at = (k, corner // 2, corner % 2)
                ref[k] = (keep_ref[at] + received_ref[at].astype(jnp.float32)).astype(ref.dtype)

    shape = (squares, held, width)
    return call(
        kernel, [(shape, jnp.float32)] + [(shape, jnp.bfloat16)] * 3, keep, received
    )


def line_messages(own, received, gain, each):
    squares, held, width = own.shape

    def kernel(own_ref, x_ref, y_ref, far_ref, gain_ref, sum_ref, *message_refs):
        gain = gain_ref[...]
        high = gain.astype(jnp.bfloat16).astype(jnp.float32)
        row = lax.broadcasted_iota(jnp.int32, (held, width), 0)
        row = row - jnp.where(lax.axis_index("ctx") % 2 == 0, each, 0)
        for k in range(squares):
            total = own_ref[k]
            for ref in (x_ref, y_ref, far_ref):
                total = total + ref[k].astype(jnp.float32)
            if k == 0:
                sum_ref[...] = total
            else:
                total = jnp.where(row == 0, high, jnp.where(row == 1, gain - high, total))
                message_refs[k - 1][...] = total.astype(jnp.bfloat16)

    return call(
        kernel,
        [((held, width), jnp.float32)] + [((held, width), jnp.bfloat16)] * (squares - 1),
        own,
        *received,
        gain,
    )


def finish(own, gain, received, each, factor):
    held, width = own.shape

    def kernel(own_ref, gain_ref, *refs):
        received_refs, (down_ref, out_ref) = refs[:-2], refs[-2:]
        is_first = lax.axis_index("ctx") % 2 == 0
        total, gain = own_ref[...], gain_ref[...]
        for ref in received_refs:
            terms = ref[...].astype(jnp.float32)
            total = total + terms
            high = jnp.where(is_first, terms[each : each + 1], terms[:1])
            gain = gain + (high + jnp.where(is_first, terms[each + 1 : each + 2], terms[1:2]))
        down_ref[...] = jnp.where(is_first, total[:each], total[held - each :]) * factor
        out_ref[...] = (gain * factor).reshape(width)

    return call(
        kernel,
        [((each, width), jnp.float32), ((width,), jnp.float32)],
        own,
        gain,
        *received,
    )


def body(tokens, cotangent, norm_gain, conv_weight, up_weight, down_weight, contig_first_bins):
    seqs, bins, width = tokens.shape
    ctx_count = lax.axis_size("ctx")
    data_count = lax.axis_size("dp")
    squares = ctx_count // 8
    gain = norm_gain.reshape(1, width)


    def prepared(tokens, cotangent, before, after_):
        normed = prepare(before, tokens, after_, gain, contig_first_bins)
        return (tokens, cotangent, before, after_, *normed)

    (conv_pieces, up_pieces, down_pieces), extra = gather(
        conv_weight, up_weight, down_weight, tokens, cotangent, prepared
    )
    tokens, cotangent, before, after_, taps, scaled, inverse = extra
    conv = assemble_conv(conv_pieces, conv_weight.shape[0])
    mixed = convolve(taps, tokens, conv)
    up = assemble_up(up_pieces, *up_weight.shape)
    mixed = after(mixed, *down_pieces)
    pre, share, hidden, total = expand(mixed, up, cotangent)
    slope = slopes(taps, before, after_, conv, up, pre, share)
    keep, send = relative_blocks(total)
    down = assemble_down(down_pieces, down_weight.shape[0])
    own_line, *others = chip_sums(keep, after(swap(send, 1), down))
    received = [swap(v, mask) for v, mask in zip(others, (2, 4, 6))]
    mixed_grad, normed_grad, gain_term = backward(
        before, cotangent, after_, slope, down, up, conv, scaled, contig_first_bins
    )
    output, input_grad = finish_rows(
        mixed, hidden, down, mixed_grad, normed_grad, scaled, inverse, gain
    )
    for mask in (1, 2, 4):
        if mask == 4:
            gain_term = after(gain_term, output)
        gain_term = gain_term + swap(gain_term, mask)
    factor = float(ctx_count * data_count * bins * seqs) ** (-0.5)
    each = total.shape[0] // ctx_count
    own_sum, *messages = line_messages(own_line, received, gain_term, each)
    arrived = [swap(message, 8 * (k + 1)) for k, message in enumerate(messages)]
    down_part, gain_all = finish(own_sum, gain_term, arrived, each, factor)
    gain_part = gain_all
    if data_count > 1:
        width_part = width // data_count
        down_part = lax.psum_scatter(down_part, "dp", scatter_dimension=1, tiled=True)
        gain_part = lax.psum(gain_part, "dp")
        at = lax.axis_index("dp") * width_part
        gain_part = lax.dynamic_slice_in_dim(gain_part, at, width_part)
    return output, input_grad, down_part, gain_part


def solution(mesh):
    placed = (
        P("dp", "ctx", None),
        P("dp", "ctx", None),
        P(),
        P(None, "ctx", None),
        P("ctx", None),
        P("ctx", None),
        P(),
    )
    return jax.shard_map(
        body,
        mesh=mesh,
        in_specs=placed,
        out_specs=(P("dp", "ctx", None), P("dp", "ctx", None), P("ctx", "dp"), P("dp")),
        check_vma=False,
    )
```

```python
import jax
import jax.numpy as jnp
from jax import lax
from jax.experimental import pallas as pl
from jax.experimental.pallas import tpu as pltpu
from jax.sharding import PartitionSpec as P

DILATION_BINS = 64


root_half = 0.7071067811865476
inv_root_two_pi = 0.3989422804014327


def swap(value, mask):
    devices = lax.axis_size("ctx")
    return lax.ppermute(value, "ctx", [(i, i ^ mask) for i in range(devices)])


def place():
    me = lax.axis_index("ctx")
    return me % 2, (me // 2) % 2, (me // 4) % 2, me // 8


def after(value, *others):
    return lax.optimization_barrier((value,) + others)[0]


VMEM = pl.BlockSpec(memory_space=pltpu.VMEM)
FIRST, SECOND, THIRD, LAST = 5000000000, 2000000000, 4500000000, 40000000000
PARAMS = pltpu.CompilerParams(vmem_limit_bytes=20 * 1024 * 1024)

SMEM = pl.BlockSpec(memory_space=pltpu.SMEM)


def call(kernel, outs, *args, smem=(), scratch=(), cost=1):
    shapes = [jax.ShapeDtypeStruct(shape, dtype) for shape, dtype in outs]
    return pl.pallas_call(
        kernel,
        out_shape=shapes,
        in_specs=[SMEM if i in smem else VMEM for i in range(len(args))],
        out_specs=[VMEM] * len(shapes),
        scratch_shapes=list(scratch),
        compiler_params=PARAMS,
        cost_estimate=pl.CostEstimate(flops=cost, bytes_accessed=1, transcendentals=0),
    )(*args)


def segment_of(position, starts_ref):
    segment = jnp.zeros_like(position)
    for i in range(starts_ref.shape[0]):
        segment = segment + jnp.where(position >= starts_ref[i], 1, 0)
    return segment


def masks_at(first, rows, starts_ref, overall):
    position = first + lax.broadcasted_iota(jnp.int32, (rows, 1), 0)
    segment = segment_of(position, starts_ref)
    left = (position >= DILATION_BINS) & (segment_of(position - DILATION_BINS, starts_ref) == segment)
    right = (position + DILATION_BINS < overall) & (
        segment_of(position + DILATION_BINS, starts_ref) == segment
    )
    return left, right


def column_blocks(width):
    return [slice(0, width)]


def prepare(before, tokens, after_, gain, starts):
    seqs, bins, width = tokens.shape
    reach = DILATION_BINS
    overall = bins * lax.axis_size("ctx")

    def kernel(before_ref, tokens_ref, after_ref, gain_ref, starts_ref, taps_ref, scaled_ref, inverse_ref):
        first = lax.axis_index("ctx") * bins - reach
        left, right = masks_at(first, bins + 2 * reach, starts_ref, overall)
        for s in range(seqs):
            parts = []
            for ref in (before_ref, tokens_ref, after_ref):
                value = (tokens_ref[s] if ref is tokens_ref else ref[s, : 2 * reach]).astype(jnp.float32)
                inverse = lax.rsqrt(jnp.mean(value * value, axis=1, keepdims=True) + 1e-05)
                scaled = value * inverse
                if ref is tokens_ref:
                    scaled_ref[s] = scaled
                    inverse_ref[s] = inverse
                parts.append(scaled * gain_ref[...])
            normed = jnp.concatenate(parts, axis=0)
            rows = bins + 2 * reach
            taps_ref[s, :, :width] = jnp.where(left, normed[:rows], 0.0).astype(jnp.bfloat16)
            taps_ref[s, :, width : 2 * width] = normed[reach : reach + rows].astype(jnp.bfloat16)
            taps_ref[s, :, 2 * width :] = jnp.where(right, normed[2 * reach :], 0.0).astype(
                jnp.bfloat16
            )

    return call(
        kernel,
        [
            ((seqs, bins + 2 * reach, 3 * width), jnp.bfloat16),
            ((seqs, bins, width), jnp.float32),
            ((seqs, bins, 1), jnp.float32),
        ],
        before,
        tokens,
        after_,
        gain,
        starts,
        smem=(4,),
    )


def convolve(taps, tokens, conv):
    seqs, bins, width = tokens.shape
    reach = DILATION_BINS

    def kernel(taps_ref, tokens_ref, conv_ref, mixed_ref):
        for s in range(seqs):
            for at in column_blocks(width):
                mixed_ref[s, :, at] = tokens_ref[s, :, at].astype(jnp.float32) + jnp.dot(
                    taps_ref[s, reach : reach + bins],
                    conv_ref[:, at],
                    preferred_element_type=jnp.float32,
                )

    return call(
        kernel, [((seqs, bins, width), jnp.float32)], taps, tokens, conv.reshape(-1, width)
    )[0]


def expand(mixed, up, cotangent):
    seqs, bins, width = cotangent.shape
    hidden_width = up.shape[1]

    def kernel(mixed_ref, up_ref, cotangent_ref, pre_ref, share_ref, hidden_ref, total_ref):
        for s in range(seqs):
            low = mixed_ref[s].astype(jnp.bfloat16)
            for at in column_blocks(hidden_width):
                pre = jnp.dot(low, up_ref[:, at], preferred_element_type=jnp.float32)
                share = 0.5 * (1.0 + lax.erf(pre * root_half))
                hidden = (pre * share).astype(jnp.bfloat16)
                pre_ref[s, :, at] = pre
                share_ref[s, :, at] = share
                hidden_ref[s, :, at] = hidden
                term = lax.dot_general(
                    hidden,
                    cotangent_ref[s],
                    (((0,), (0,)), ((), ())),
                    preferred_element_type=jnp.float32,
                )
                if s == 0:
                    total_ref[at, :] = term
                else:
                    total_ref[at, :] += term

    return call(
        kernel,
        [
            ((seqs, bins, hidden_width), jnp.float32),
            ((seqs, bins, hidden_width), jnp.float32),
            ((seqs, bins, hidden_width), jnp.bfloat16),
            ((hidden_width, width), jnp.float32),
        ],
        mixed,
        up,
        cotangent,
    )


def slopes(taps, before, after_, conv, up, pre, share):
    seqs, bins, hidden_width = pre.shape
    width = before.shape[2]
    reach = DILATION_BINS
    rows = bins + 2 * reach

    def bell(value):
        return value * jnp.exp(-0.5 * value * value) * inv_root_two_pi

    def kernel(taps_ref, before_ref, after_ref, conv_ref, up_ref, pre_ref, share_ref, slope_ref, mixed):
        for s in range(seqs):
            edges = jnp.concatenate([taps_ref[s, :reach], taps_ref[s, reach + bins :]], axis=0)
            tokens = jnp.concatenate([before_ref[s, reach : 2 * reach], after_ref[s, :reach]], axis=0)
            for at in column_blocks(width):
                mixed[:, at] = (
                    tokens[:, at].astype(jnp.float32)
                    + jnp.dot(edges, conv_ref[:, at], preferred_element_type=jnp.float32)
                ).astype(jnp.bfloat16)
            for at in column_blocks(hidden_width):
                edge = jnp.dot(mixed[...], up_ref[:, at], preferred_element_type=jnp.float32)
                slope = 0.5 * (1.0 + lax.erf(edge * root_half)) + bell(edge)
                slope_ref[s, :reach, at] = slope[:reach]
                slope_ref[s, reach : reach + bins, at] = share_ref[s, :, at] + bell(pre_ref[s, :, at])
                slope_ref[s, reach + bins :, at] = slope[reach:]

    return call(
        kernel,
        [((seqs, rows, hidden_width), jnp.float32)],
        taps,
        before,
        after_,
        conv.reshape(-1, width),
        up,
        pre,
        share,
        scratch=[pltpu.VMEM((2 * reach, width), jnp.bfloat16)],
    )[0]


def backward(before, cotangent, after_, slope, down, up, conv, scaled, starts):
    seqs, bins, width = cotangent.shape
    hidden_width = up.shape[1]
    reach = DILATION_BINS
    rows = bins + 2 * reach
    overall = bins * lax.axis_size("ctx")
    by_rows = (((1,), (1,)), ((), ()))

    def kernel(
        before_ref,
        cotangent_ref,
        after_ref,
        slope_ref,
        down_ref,
        up_ref,
        conv_ref,
        scaled_ref,
        starts_ref,
        mixed_grad_ref,
        normed_grad_ref,
        gain_term_ref,
        pre_grad,
        mixed_grad,
    ):
        first = lax.axis_index("ctx") * bins
        left, right = masks_at(first, bins, starts_ref, overall)
        for s in range(seqs):
            cot = jnp.concatenate(
                [before_ref[s, 2 * reach :], cotangent_ref[s], after_ref[s, 2 * reach :]], axis=0
            )
            for at in column_blocks(hidden_width):
                hidden_grad = lax.dot_general(
                    cot, down_ref[at, :], by_rows, preferred_element_type=jnp.float32
                )
                pre_grad[:, at] = (hidden_grad * slope_ref[s, :, at]).astype(jnp.bfloat16)
            for at in column_blocks(width):
                mixed_grad[:, at] = cot[:, at].astype(jnp.float32) + lax.dot_general(
                    pre_grad[...], up_ref[at, :], by_rows, preferred_element_type=jnp.float32
                )
            following = jnp.where(right, mixed_grad[2 * reach :, :], 0.0).astype(jnp.bfloat16)
            center = mixed_grad[reach : reach + bins, :].astype(jnp.bfloat16)
            preceding = jnp.where(left, mixed_grad[:bins, :], 0.0).astype(jnp.bfloat16)
            mixed_grad_ref[s] = mixed_grad[reach : reach + bins, :]
            for at in column_blocks(width):
                normed_grad = (
                    lax.dot_general(following, conv_ref[0, at, :], by_rows, preferred_element_type=jnp.float32)
                    + lax.dot_general(center, conv_ref[1, at, :], by_rows, preferred_element_type=jnp.float32)
                    + lax.dot_general(preceding, conv_ref[2, at, :], by_rows, preferred_element_type=jnp.float32)
                )
                normed_grad_ref[s, :, at] = normed_grad
                term = jnp.sum(normed_grad * scaled_ref[s, :, at], axis=0, keepdims=True)
                if s == 0:
                    gain_term_ref[:, at] = term
                else:
                    gain_term_ref[:, at] += term

    return call(
        kernel,
        [
            ((seqs, bins, width), jnp.float32),
            ((seqs, bins, width), jnp.float32),
            ((1, width), jnp.float32),
        ],
        before,
        cotangent,
        after_,
        slope,
        down,
        up,
        conv,
        scaled,
        starts,
        smem=(8,),
        scratch=[
            pltpu.VMEM((rows, hidden_width), jnp.bfloat16),
            pltpu.VMEM((rows, width), jnp.float32),
        ],
    )


def finish_rows(mixed, hidden, down, mixed_grad, normed_grad, scaled, inverse, gain):
    seqs, bins, _ = hidden.shape
    width = down.shape[1]

    def kernel(
        mixed_ref,
        hidden_ref,
        down_ref,
        mixed_grad_ref,
        normed_grad_ref,
        scaled_ref,
        inverse_ref,
        gain_ref,
        out_ref,
        grad_ref,
    ):
        for s in range(seqs):
            scaled = scaled_ref[s]
            scaled_grad = normed_grad_ref[s] * gain_ref[...]
            inner = jnp.mean(scaled_grad * scaled, axis=1, keepdims=True)
            grad_ref[s] = (
                mixed_grad_ref[s] + inverse_ref[s] * (scaled_grad - scaled * inner)
            ).astype(jnp.bfloat16)
            for at in column_blocks(width):
                out_ref[s, :, at] = (
                    mixed_ref[s, :, at]
                    + jnp.dot(hidden_ref[s], down_ref[:, at], preferred_element_type=jnp.float32)
                ).astype(jnp.bfloat16)

    return call(
        kernel,
        [((seqs, bins, width), jnp.bfloat16)] * 2,
        mixed,
        hidden,
        down,
        mixed_grad,
        normed_grad,
        scaled,
        inverse,
        gain,
    )


def stack(pieces, cost=1):
    def kernel(*refs):
        for i in range(len(pieces)):
            refs[-1][i] = refs[i][...]

    shape = (len(pieces),) + pieces[0].shape
    return call(kernel, [(shape, pieces[0].dtype)], *pieces, cost=cost)[0]


def join(*pieces, cost=1):
    ends = [sum(piece.shape[0] for piece in pieces[: i + 1]) for i in range(len(pieces))]

    def kernel(*refs):
        for ref, end in zip(refs[:-1], ends):
            refs[-1][end - ref.shape[0] : end] = ref[...]

    shape = (ends[-1],) + pieces[0].shape[1:]
    return call(kernel, [(shape, pieces[0].dtype)], *pieces, cost=cost)[0]


def join_rows(pieces, rows, cost=1):
    ends = [sum(stop - start for _, start, stop in pieces[: i + 1]) for i in range(len(pieces))]
    held, width = pieces[0][0].shape[1:]

    def kernel(*refs):
        for ref, (_, start, stop), end in zip(refs[:-2], pieces, ends):
            at = slice(end - (stop - start), end)
            refs[-2][at] = ref[start:stop, :rows]
            refs[-1][at] = ref[start:stop, rows:]

    shapes = [(ends[-1], rows, width), (ends[-1], held - rows, width)]
    arrays = [piece[0] for piece in pieces]
    return call(kernel, [(shape, arrays[0].dtype) for shape in shapes], *arrays, cost=cost)


def join_parts(*pieces):
    ends = [sum(stop - start for _, start, stop in pieces[: i + 1]) for i in range(len(pieces))]

    def kernel(*refs):
        for ref, (_, start, stop), end in zip(refs[:-1], pieces, ends):
            refs[-1][end - (stop - start) : end] = ref[start:stop]

    shape = (ends[-1],) + pieces[0][0].shape[1:]
    return call(kernel, [(shape, pieces[0][0].dtype)], *[p[0] for p in pieces])[0]


def neighbours(tokens, cotangent):
    devices = lax.axis_size("ctx")
    pairs = [(i, i + 1) for i in range(1, devices - 1, 2)]
    pairs += [(j, i) for i, j in pairs]
    far, near = 2 * DILATION_BINS, DILATION_BINS
    seqs, bins, width = tokens.shape

    def cut(tokens_ref, cotangent_ref, last_ref, leading_ref):
        last_ref[:, :far] = tokens_ref[:, bins - far :]
        last_ref[:, far:] = cotangent_ref[:, bins - near :]
        leading_ref[:, :far] = tokens_ref[:, :far]
        leading_ref[:, far:] = cotangent_ref[:, :near]

    def kernel(tokens_ref, cotangent_ref, inner_ref, outer_ref):
        is_first = lax.axis_index("ctx") % 2 == 0

        @pl.when(is_first)
        def _():
            cut(tokens_ref, cotangent_ref, inner_ref, outer_ref)

        @pl.when(jnp.logical_not(is_first))
        def _():
            cut(tokens_ref, cotangent_ref, outer_ref, inner_ref)

    edge = ((seqs, far + near, width), tokens.dtype)
    inner, outer = call(kernel, [edge, edge], tokens, cotangent)
    return inner, lax.ppermute(outer, "ctx", pairs)


def in_order(inner, outer):
    def kernel(inner_ref, outer_ref, before_ref, after_ref):
        is_first = lax.axis_index("ctx") % 2 == 0

        @pl.when(is_first)
        def _():
            before_ref[...] = outer_ref[...]
            after_ref[...] = inner_ref[...]

        @pl.when(jnp.logical_not(is_first))
        def _():
            before_ref[...] = inner_ref[...]
            after_ref[...] = outer_ref[...]

    return call(kernel, [(inner.shape, inner.dtype)] * 2, inner, outer)


def line_slots(squares):
    def slots(z):
        slot, first, count = 0, 0, 2
        while first < squares:
            for corner in range(4):
                last = corner == 3 and first + count == squares
                for k in range(count):
                    source = square_of(z, first + k, squares)
                    yield int(last), k if last else slot, source, corner // 2, corner % 2
                    slot += 1
            first, count = first + count, first + count

    return slots


def assemble_conv(pieces, taps):
    squares = lax.axis_size("ctx") // 8
    width = pieces[0].shape[-1]
    rows = pieces[0].shape[-2] // taps

    def kernel(*refs):
        out = refs[-1]
        core, x, y, z = place()
        for dc in range(2):
            for last, slot, source, dy, dx in line_slots(squares)(z):
                for t in range(taps):
                    part = refs[2 * last + dc][slot, t * rows : (t + 1) * rows]
                    out[t, source, y ^ dy, x ^ dx, core ^ dc] = part

    out = call(kernel, [((taps, squares, 2, 2, 2, rows, width), pieces[0].dtype)], *pieces)[0]
    return out.reshape(taps, squares * 8 * rows, width)


def assemble_down(pieces, rows):
    squares = lax.axis_size("ctx") // 8
    width = pieces[0].shape[-1]

    def kernel(*refs):
        out, wide = refs[-2:]
        core, x, y, z = place()
        is_first = core == 0
        for last, slot, source, dy, dx in line_slots(squares)(z):
            mine = refs[2 * last][slot, :rows].astype(jnp.float32)
            theirs = refs[2 * last + 1][slot, :rows].astype(jnp.float32)
            wide[:rows] = jnp.where(is_first, mine, theirs)
            wide[rows:] = jnp.where(is_first, theirs, mine)
            out[source, y ^ dy, x ^ dx] = wide[...].astype(jnp.bfloat16)

    out = call(
        kernel,
        [((squares, 2, 2, 2 * rows, width), pieces[0].dtype)],
        *pieces,
        scratch=[pltpu.VMEM((2 * rows, width), jnp.float32)],
    )[0]
    return out.reshape(squares * 8 * rows, width)


def assemble_up(pieces, rows, width):
    squares = lax.axis_size("ctx") // 8

    def kernel(*refs):
        out = refs[-1]
        core, x, y, z = place()
        for piece, index, source, dy, dx, dc in up_slots(squares)(z):
            out[source, y ^ dy, x ^ dx, core ^ dc] = refs[piece][index]

    out = call(kernel, [((squares, 2, 2, 2, rows, width), pieces[0].dtype)], *pieces)[0]
    return out.reshape(squares * 8 * rows, width)


def line_masks(squares):
    return [8 << i for i in reversed(range(squares.bit_length() - 1))]


def square_of(z, slot, squares):
    for i, mask in enumerate(line_masks(squares)):
        if slot >> i & 1:
            z = z ^ (mask // 8)
    return z


def up_slots(squares):
    def slots(z):
        for core in range(2):
            for k in range(squares):
                for corner in range(4):
                    source = square_of(z, k, squares)
                    yield core, (4 * k + corner,), source, corner // 2, corner % 2, core

    return slots


def all_after(values, others):
    count = len(values)
    return lax.optimization_barrier((*values, *others))[:count]


def load(*arrays):
    count = len(arrays)

    def kernel(*refs):
        ins, outs, sem = refs[:count], refs[count:-1], refs[-1]
        copies = [pltpu.make_async_copy(i, o, sem.at[at]) for at, (i, o) in enumerate(zip(ins, outs))]
        for copy in copies:
            copy.start()
        for copy in copies:
            copy.wait()

    return pl.pallas_call(
        kernel,
        out_shape=[jax.ShapeDtypeStruct(a.shape, a.dtype) for a in arrays],
        in_specs=[pl.BlockSpec(memory_space=pltpu.HBM)] * count,
        out_specs=[VMEM] * count,
        scratch_shapes=[pltpu.SemaphoreType.DMA((count,))],
        compiler_params=PARAMS,
        cost_estimate=pl.CostEstimate(flops=1, bytes_accessed=1, transcendentals=0),
    )(*arrays)


def pack(conv_parts, down_parts, cost):
    taps, rows, width = conv_parts[0].shape
    down_rows = down_parts[0].shape[0]
    held = -(-(taps * rows + down_rows) // 16) * 16
    count = len(conv_parts)

    def kernel(*refs):
        out = refs[-1]
        for i in range(count):
            for t in range(taps):
                out[i, t * rows : (t + 1) * rows] = refs[i][t]
            out[i, taps * rows : taps * rows + down_rows] = refs[count + i][...]

    arrays = (*conv_parts, *down_parts)
    return call(kernel, [((count, held, width), conv_parts[0].dtype)], *arrays, cost=cost)[0]


def gather(conv, up, down, tokens, cotangent, prepared):
    first, *rest = line_masks(lax.axis_size("ctx") // 8)
    rows = conv.shape[0] * conv.shape[1]
    new, down_new = swap(conv, first), swap(down, first)
    up_new = [swap(up, mask) for mask in (2, 4, 6)]
    inner, outer = neighbours(*all_after((tokens, cotangent), (up_new[0],)))
    conv, up, down = load(conv, up, down)
    new, down_new, *up_new = all_after((new, down_new, *up_new), ())
    part = held = pack([conv, new], [down, down_new], cost=FIRST)
    up_held = stack([up] + up_new, cost=SECOND)
    pieces, late = [], None
    for mask, next_mask in zip([first] + rest, rest + [None]):
        count = part.shape[0]
        if late is None:
            to_x, to_y = part, part
        else:
            old, old_x, old_y = late
            to_x = join_parts((part, 0, count), (old_y, old // 2, old))
            to_y = join_parts((part, 0, count), (old_x, 0, old // 2))
        by_x, by_y, received = swap(to_x, 2), swap(to_y, 4), swap(up_held, mask)
        other = swap(inner, 1) if next_mask is None else swap(held, next_mask)
        up_held = join(up_held, received)
        if next_mask is None:
            outer = stack([outer], cost=THIRD)
        phase = (part, held, up_held, by_x, by_y, other)
        if next_mask is None:
            part, held, up_held, by_x, by_y, other, outer = all_after((*phase, outer), ())
        else:
            part, held, up_held, by_x, by_y, other = all_after(phase, ())
        if late is not None:
            pieces += [(by_y, count, count + old // 2), (by_x, count, count + old - old // 2)]
        pieces += [(part, 0, count), (by_x, 0, count), (by_y, 0, count)]
        late = (count, by_x, by_y)
        if next_mask is not None:
            held, part = join(held, other), other
    half = count // 2
    far_first = swap(join_parts((by_x, 0, half)), 4)
    far_second = swap(join_parts((by_y, half, count)), 2)
    extra = prepared(tokens, cotangent, *in_order(other, outer[0]))
    far_first = after(far_first, extra[4])
    most = join_rows(pieces, rows)
    last = join_rows([(far_first, 0, half), (far_second, 0, count - half)], rows, cost=LAST)
    pieces = [(most[0], last[0]), (up_held,), (most[1], last[1])]
    return [[both for p in piece for both in (p, swap(p, 1))] for piece in pieces], extra


def core_rows(rows):
    start = (rows // 2 - 2) // 8 * 8
    return start, rows - start


def relative_blocks(total):
    squares = lax.axis_size("ctx") // 8
    rows, width = total.shape[0] // (4 * squares), total.shape[1]
    start, held = core_rows(rows)
    blocks = total.reshape(squares, 2, 2, rows, width)

    def kernel(blocks_ref, keep_ref, send_ref):
        core, x, y, z = place()
        keep = pl.ds(pl.multiple_of(core * start, 8), held)
        send = pl.ds(pl.multiple_of((1 - core) * start, 8), held)
        for k in range(squares):
            for dy in range(2):
                for dx in range(2):
                    keep_ref[k, dy, dx] = blocks_ref[z ^ k, y ^ dy, x ^ dx, keep, :]
                    send_ref[k, dy, dx] = blocks_ref[z ^ k, y ^ dy, x ^ dx, send, :].astype(jnp.bfloat16)

    shape = (squares, 2, 2, held, width)
    return call(kernel, [(shape, jnp.float32), (shape, jnp.bfloat16)], blocks)


def chip_sums(keep, received):
    squares, _, _, held, width = keep.shape

    def kernel(keep_ref, received_ref, own_ref, x_ref, y_ref, far_ref):
        for k in range(squares):
            for corner, ref in enumerate((own_ref, x_ref, y_ref, far_ref)):
                at = (k, corner // 2, corner % 2)
                ref[k] = (keep_ref[at] + received_ref[at].astype(jnp.float32)).astype(ref.dtype)

    shape = (squares, held, width)
    return call(
        kernel, [(shape, jnp.float32)] + [(shape, jnp.bfloat16)] * 3, keep, received
    )


def line_messages(own, received, gain, each):
    squares, held, width = own.shape

    def kernel(own_ref, x_ref, y_ref, far_ref, gain_ref, sum_ref, *message_refs):
        gain = gain_ref[...]
        high = gain.astype(jnp.bfloat16).astype(jnp.float32)
        row = lax.broadcasted_iota(jnp.int32, (held, width), 0)
        row = row - jnp.where(lax.axis_index("ctx") % 2 == 0, each, 0)
        for k in range(squares):
            total = own_ref[k]
            for ref in (x_ref, y_ref, far_ref):
                total = total + ref[k].astype(jnp.float32)
            if k == 0:
                sum_ref[...] = total
            else:
                total = jnp.where(row == 0, high, jnp.where(row == 1, gain - high, total))
                message_refs[k - 1][...] = total.astype(jnp.bfloat16)

    return call(
        kernel,
        [((held, width), jnp.float32)] + [((held, width), jnp.bfloat16)] * (squares - 1),
        own,
        *received,
        gain,
    )


def finish(own, gain, received, each, factor):
    held, width = own.shape

    def kernel(own_ref, gain_ref, *refs):
        received_refs, (down_ref, out_ref) = refs[:-2], refs[-2:]
        is_first = lax.axis_index("ctx") % 2 == 0
        total, gain = own_ref[...], gain_ref[...]
        for ref in received_refs:
            terms = ref[...].astype(jnp.float32)
            total = total + terms
            high = jnp.where(is_first, terms[each : each + 1], terms[:1])
            gain = gain + (high + jnp.where(is_first, terms[each + 1 : each + 2], terms[1:2]))
        down_ref[...] = jnp.where(is_first, total[:each], total[held - each :]) * factor
        out_ref[...] = (gain * factor).reshape(width)

    return call(
        kernel,
        [((each, width), jnp.float32), ((width,), jnp.float32)],
        own,
        gain,
        *received,
    )


def body(tokens, cotangent, norm_gain, conv_weight, up_weight, down_weight, contig_first_bins):
    seqs, bins, width = tokens.shape
    ctx_count = lax.axis_size("ctx")
    data_count = lax.axis_size("dp")
    squares = ctx_count // 8
    gain = norm_gain.reshape(1, width)


    def prepared(tokens, cotangent, before, after_):
        normed = prepare(before, tokens, after_, gain, contig_first_bins)
        return (tokens, cotangent, before, after_, *normed)

    (conv_pieces, up_pieces, down_pieces), extra = gather(
        conv_weight, up_weight, down_weight, tokens, cotangent, prepared
    )
    tokens, cotangent, before, after_, taps, scaled, inverse = extra
    conv = assemble_conv(conv_pieces, conv_weight.shape[0])
    mixed = convolve(taps, tokens, conv)
    up = assemble_up(up_pieces, *up_weight.shape)
    mixed = after(mixed, *down_pieces)
    pre, share, hidden, total = expand(mixed, up, cotangent)
    slope = slopes(taps, before, after_, conv, up, pre, share)
    keep, send = relative_blocks(total)
    down = assemble_down(down_pieces, down_weight.shape[0])
    own_line, *others = chip_sums(keep, after(swap(send, 1), slope, down))
    received = [swap(v, mask) for v, mask in zip(others, (2, 4, 6))]
    mixed_grad, normed_grad, gain_term = backward(
        before, cotangent, after_, slope, down, up, conv, scaled, contig_first_bins
    )
    output, input_grad = finish_rows(
        mixed, hidden, down, mixed_grad, normed_grad, scaled, inverse, gain
    )
    for mask in (1, 2, 4):
        gain_term = gain_term + swap(gain_term, mask)
    factor = float(ctx_count * data_count * bins * seqs) ** (-0.5)
    each = total.shape[0] // ctx_count
    own_sum, *messages = line_messages(own_line, received, gain_term, each)
    arrived = [swap(message, 8 * (k + 1)) for k, message in enumerate(messages)]
    down_part, gain_all = finish(own_sum, gain_term, arrived, each, factor)
    gain_part = gain_all
    if data_count > 1:
        width_part = width // data_count
        down_part = lax.psum_scatter(down_part, "dp", scatter_dimension=1, tiled=True)
        gain_part = lax.psum(gain_part, "dp")
        at = lax.axis_index("dp") * width_part
        gain_part = lax.dynamic_slice_in_dim(gain_part, at, width_part)
    return output, input_grad, down_part, gain_part


def solution(mesh):
    placed = (
        P("dp", "ctx", None),
        P("dp", "ctx", None),
        P(),
        P(None, "ctx", None),
        P("ctx", None),
        P("ctx", None),
        P(),
    )
    return jax.shard_map(
        body,
        mesh=mesh,
        in_specs=placed,
        out_specs=(P("dp", "ctx", None), P("dp", "ctx", None), P("ctx", "dp"), P("dp")),
        check_vma=False,
    )
```
